32 devices in a mesh: func: 16 (over z, y, x), rep: 2 (over core).
Axes of the slice: x: 2, y: 2, z: 4, core: 2. Of those that a mesh axis runs over, the one named last changes fastest.
Arguments:
- orbitals: bfloat16 [1536, 32, 1024], P('func', 'rep'), may hold values from -6 to 6
- centres: int32 [1536, 3], P('func'), may hold values from 0 to 463, as said below
- potential: float32 [512, 128, 128], P('func'), may hold values from -6 to 6
- kernel: bfloat16 [2, 9216, 128], P('rep', 'func'), may hold values from -0.15625 to 0.15625
- kernel_cols: int32 [12, 12], replicated, may hold values from 0 to 11, as said below
- hamiltonian: bfloat16 [2, 9216, 128], P('rep', 'func'), may hold values from -0.15625 to 0.15625
- intersection_cols: int32 [12, 12], replicated, may hold values from 0 to 11, as said below
Outputs:
- gradient: bfloat16 [1536, 32, 1024], P('func', 'rep')
The draws below stay inside these ranges and needn't reach their ends.
Inputs may be any that keep to these rules, and one draw needn't show every extreme that they name: centres[f, 0] = 32 * g + o with 0 <= g <= 14 and 0 <= o < 16; centres[f, 1] and centres[f, 2] lie in 0 to 127. In each aligned block of 96 rows, at most 14 rows share the same g, and in some such block of every draw exactly 14 do. Every draw has a row with g = 14, o = 15, centres[f, 1] = 127 and centres[f, 2] = 0. `kernel_cols`: each row names 12 distinct column blocks, the first being the row's own block. `intersection_cols`: each row names 12 distinct column blocks, the first being the row's own block.
All inputs are finite; a program needn't handle non-finite values.
Results may differ from the reference program's by a relative error of at most 0.006.
Values may be sent and summed in bfloat16 or wider, within the bound.
No kernel may reach another device: no remote copies, remote signals or barrier semaphores. Data moves between devices by JAX's collectives and lax.ppermute only.
A program may use at most 256 MiB of HBM per device.

```python
import jax
import jax.numpy as jnp
from jax import lax

BOX = 32
BLK = 128
NNZB = 12
NF = 1536
GXY = 128
NB = 12
GZ = 512
CAP = 14
HALF_ROWS = 9216
N_FUNC = 16
N_REP = 2


def block_pattern(key):
    scores = jax.random.randint(key, (NB, NB), 0, 1 << 20) * NB + jnp.arange(NB)[None, :]
    own_block = jnp.arange(NB)[:, None] == jnp.arange(NB)[None, :]
    scores = jnp.where(own_block, -1, scores)
    return jnp.argsort(scores, axis=1)[:, :NNZB].astype(jnp.int32)


def draw_kernel_cols(key, part):
    key = jax.random.fold_in(key, 5)
    return block_pattern(key)


def draw_intersection_cols(key, part):
    key = jax.random.fold_in(key, 7)
    return block_pattern(key)


def draw_centres(key, part):
    key = jax.random.fold_in(key, 11)
    keys = jax.random.split(key, 6)
    owned = NF // N_FUNC
    regions_free = N_FUNC - 1
    lowest = CAP // 2
    owners = jnp.arange(N_FUNC)
    group_size_list = jax.random.randint(keys[0], (N_FUNC,), lowest, CAP + 1)
    chosen = jax.random.randint(keys[1], (), 0, N_FUNC)
    group_size_list = jnp.where(owners == chosen, CAP, group_size_list)
    bases = jax.random.randint(keys[2], (N_FUNC,), 0, regions_free)
    bases = jnp.where(owners == chosen, regions_free - 1, bases)
    scores = jax.random.randint(keys[3], (N_FUNC, owned), 0, 1 << 20) * owned + jnp.arange(owned)[None, :]
    ranks = jnp.argsort(jnp.argsort(scores, axis=1), axis=1)
    regions = (bases[:, None] + ranks // group_size_list[:, None]) % regions_free
    marked = (owners[:, None] == chosen) & (ranks == 0)
    inner = jax.random.randint(keys[4], (N_FUNC, owned), 0, BOX // N_REP)
    inner = jnp.where(marked, BOX // N_REP - 1, inner)
    start_z = regions * BOX + inner
    start_xy = jax.random.randint(keys[5], (N_FUNC, owned, 2), 0, GXY)
    box_corner_point = jnp.array([GXY - 1, 0], dtype=jnp.int32)
    start_xy = jnp.where(marked[:, :, None], box_corner_point[None, None, :], start_xy)
    joined = jnp.concatenate([start_z[:, :, None], start_xy], axis=2)
    return joined.reshape(NF, 3).astype(jnp.int32)


def level_of(key, dims, cuts, smallest, high):
    level, own = 1.0, jax.random.fold_in(key, 6)
    for dim, shards_of in cuts:
        heights = jnp.exp(jax.random.uniform(jax.random.fold_in(own, dim), (shards_of,), jnp.float32, smallest / len(cuts), high / len(cuts)))
        level = level * jnp.repeat(heights, dims[dim] // shards_of).reshape([-1 if axis == dim else 1 for axis in range(len(dims))])
    return level


def noise(own_key, shape, deviation, most, cuts=(), kind=jnp.bfloat16):
    drawn = jax.random.normal(own_key, shape, jnp.float32) * deviation
    if len(cuts) > 0:
        drawn = level_of(own_key, shape, cuts, -0.22, 0.18) * drawn
    return jnp.clip(drawn, min=-most, max=most).astype(kind)


def setup_inputs(seed: int = 0) -> dict:
    seeds = jax.random.split(jax.random.key(seed), 8)
    orbitals = noise(seeds[0], (NF, BOX, BOX * BOX), 1.0, 6.0, ((0, 16), (1, 2)))
    centres = draw_centres(jax.random.fold_in(seeds[7], 71), 0)
    potential = noise(seeds[2], (GZ, GXY, GXY), 1.0, 6.0, ((0, 16),), jnp.float32)
    kernel = noise(seeds[3], (N_REP, HALF_ROWS, BLK), (NNZB * BLK) ** -0.5, 0.15625, ((0, 2), (1, 16)))
    kernel_cols = draw_kernel_cols(jax.random.fold_in(seeds[7], 71), 0)
    hamiltonian = noise(seeds[5], (N_REP, HALF_ROWS, BLK), (NNZB * BLK) ** -0.5, 0.15625, ((0, 2), (1, 16)))
    intersection_cols = draw_intersection_cols(jax.random.fold_in(seeds[7], 71), 0)
    return {"orbitals": orbitals, "centres": centres, "potential": potential, "kernel": kernel, "kernel_cols": kernel_cols, "hamiltonian": hamiltonian, "intersection_cols": intersection_cols}


COEFF_CENTRE = -2.5
COEFF_NEAR = 4.0 / 3.0
COEFF_FAR = -1.0 / 12.0
INV_SPACING = 0.25


def laplacian(value_entries):
    edge = value_entries.shape[1]
    total = 3.0 * COEFF_CENTRE * value_entries
    for axis in (1, 2, 3):
        widths = [(0, 0), (0, 0), (0, 0), (0, 0)]
        widths[axis] = (2, 2)
        padded = jnp.pad(value_entries, widths)
        for distance, weight in ((1, COEFF_NEAR), (2, COEFF_FAR)):
            upper = lax.slice_in_dim(padded, 2 + distance, 2 + distance + edge, axis=axis)
            lower = lax.slice_in_dim(padded, 2 - distance, 2 - distance + edge, axis=axis)
            total = total + weight * (upper + lower)
    return INV_SPACING * total


def apply_blocks(blocks, cols, rows):
    grouped_rows = rows.reshape(NB, BLK, rows.shape[1])

    def one_row(index):
        taken = grouped_rows[cols[index]].astype(jnp.float32)
        return jnp.einsum("kab,kbp->ap", blocks[index].astype(jnp.float32), taken)

    return lax.map(one_row, jnp.arange(NB, dtype=jnp.int32)).reshape(NF, rows.shape[1])


def reference(orbitals, centres, potential, kernel, kernel_cols, hamiltonian, intersection_cols):
    wrapped = jnp.concatenate([potential, potential[:, :BOX - 1]], axis=1)
    wrapped = jnp.concatenate([wrapped, wrapped[:, :, :BOX - 1]], axis=2)

    def block_term(operands):
        phi_block, centre_block = operands

        def window(entry):
            cut = lax.dynamic_slice(wrapped, (entry[0], entry[1], entry[2]), (BOX, BOX, BOX))
            return cut.reshape(BOX, BOX * BOX)

        window_list = jax.vmap(window)(centre_block)
        value_entries = phi_block.astype(jnp.float32)
        potential_times_support = lax.optimization_barrier((window_list * value_entries).astype(jnp.bfloat16))
        kinetic_energy_part = -0.5 * laplacian(value_entries.reshape(BLK, BOX, BOX, BOX)).reshape(BLK, BOX, BOX * BOX)
        return (kinetic_energy_part + potential_times_support.astype(jnp.float32)).astype(jnp.bfloat16)

    hphi = lax.map(block_term, (orbitals.reshape(NB, BLK, BOX, BOX * BOX), centres.reshape(NB, BLK, 3)))
    hphi = hphi.reshape(NF, BOX * BOX * BOX)
    phi_rows = orbitals.reshape(NF, BOX * BOX * BOX)
    k_blocks = kernel.reshape(NB, NNZB, BLK, BLK)
    h_blocks = hamiltonian.reshape(NB, NNZB, BLK, BLK)
    kphi = apply_blocks(k_blocks, kernel_cols, phi_rows).astype(jnp.bfloat16)
    ydiff = (hphi.astype(jnp.float32) - apply_blocks(h_blocks, intersection_cols, kphi)).astype(jnp.bfloat16)
    gradient = apply_blocks(k_blocks, kernel_cols, ydiff).astype(jnp.bfloat16)
    return gradient.reshape(NF, BOX, BOX * BOX)
```

```python
import jax
import jax.numpy as jnp
from jax import lax
from jax.experimental import pallas as pl
from jax.experimental.pallas import tpu as pltpu
from jax.sharding import PartitionSpec as P

BOX = 32
BLK = 128
NNZB = 12
NB = 12
NF = NB * BLK
LANES = 128
ROWS = 16
GROUP = 16
COLS = 256
VMEM = 56 * 1024 * 1024

CENTRE = 90.0
NEAR = -16.0
FAR = 1.0
SCALE = 1.0 / 96.0


def planar_band():
    row = lax.broadcasted_iota(jnp.int32, (2 * COLS, COLS), 0) - LANES
    col = lax.broadcasted_iota(jnp.int32, (2 * COLS, COLS), 1)
    across = jnp.abs((row + LANES) // BOX - (col + LANES) // BOX)
    along = jnp.abs((row + LANES) % BOX - (col + LANES) % BOX)
    band = jnp.zeros((2 * COLS, COLS), jnp.float32)
    for one, other in ((across, along), (along, across)):
        band = jnp.where((one == 0) & (other == 1), NEAR, band)
        band = jnp.where((one == 0) & (other == 2), FAR, band)
    band = jnp.where((across == 0) & (along == 0), CENTRE, band)
    return band.astype(jnp.bfloat16)


def hphi_kernel(
    info, phi, halo, band, pot, out, buf, rows, win, sems
):
    planes, group, flat = phi.shape
    step = pl.program_id(0)
    total = pl.num_programs(0) * group
    x_blocks = pot.shape[2]
    span = 3 * ROWS
    flag = info[0, 3].astype(jnp.float32)

    def copies(index, slot):
        z = info[index, 0]
        first = info[index, 1] // ROWS
        out_list = []
        for k in range(3):
            block = lax.rem(first + k, 2 * x_blocks)
            out_list.append(
                pltpu.make_async_copy(
                    pot.at[block // x_blocks, pl.ds(z, planes), lax.rem(block, x_blocks)],
                    buf.at[slot, k],
                    sems.at[slot, k],
                )
            )
        return out_list

    @pl.when(step == 0)
    def _():
        for copy in copies(0, 0):
            copy.start()

    lane = lax.broadcasted_iota(jnp.int32, (8, LANES), 1)

    def one_function(f, carry):
        index = step * group + f
        slot = lax.rem(index, 2)

        @pl.when(index + 1 < total)
        def _():
            for copy in copies(index + 1, 1 - slot):
                copy.start()

        for copy in copies(index, slot):
            copy.wait()
        for z in range(planes):
            for k in range(3):
                rows[pl.ds(z * span + k * ROWS, ROWS), :] = buf[slot, k, z].astype(jnp.float32)
        shift_x = lax.rem(info[index, 1], ROWS)
        shift_y = info[index, 2]
        for z in range(planes):
            value = None
            for b in range(4):
                part = rows[pl.ds(z * span + b + shift_x, 8, stride=4), :]
                part = pltpu.roll(part, lax.rem(b * BOX + LANES - shift_y, LANES), axis=1)
                value = part if value is None else jnp.where(lane >= b * BOX, part, value)
            win[pl.ds(z * group + f, 8, stride=planes * group), :] = value
        return carry

    lax.fori_loop(0, group, one_function, 0)

    pieces = flat // COLS
    for c in range(pieces):
        low = max(0, c * COLS - LANES)
        high = min(flat, c * COLS + COLS + LANES)
        cols = slice(c * COLS, (c + 1) * COLS)
        left = phi[:, :, low:high].reshape(planes * group, high - low)
        base = low - (c * COLS - LANES)
        planar = jnp.dot(
            left, band[base : base + high - low, :], preferred_element_type=jnp.float32
        )
        level = [phi[z, :, cols].astype(jnp.float32) for z in range(planes)]
        other = [halo[h, :, cols].astype(jnp.float32) for h in range(2)]
        below = [h * flag for h in other]
        above = [h * (1.0 - flag) for h in other]
        level = below + level + above
        for z in range(planes):
            kin = planar[z * group : (z + 1) * group]
            kin = kin + NEAR * (level[z + 1] + level[z + 3]) + FAR * (level[z] + level[z + 4])
            w = jnp.concatenate(
                [
                    win[pl.ds((a * planes + z) * group, group), :]
                    for a in range(c * COLS // LANES, (c + 1) * COLS // LANES)
                ],
                axis=1,
            )
            vphi = (w * level[z + 2]).astype(jnp.bfloat16).astype(jnp.float32)
            out[z, :, cols] = (SCALE * kin + vphi).astype(jnp.bfloat16)


def make_hphi(info, phi, halo, band, pot):
    planes, owned, flat = phi.shape
    x_blocks = pot.shape[2]
    span = 3 * ROWS
    grid_spec = pltpu.PrefetchScalarGridSpec(
        num_scalar_prefetch=1,
        grid=(owned // GROUP,),
        in_specs=[
            pl.BlockSpec((planes, GROUP, flat), lambda i, s: (0, i, 0)),
            pl.BlockSpec((2, GROUP, flat), lambda i, s: (0, i, 0)),
            pl.BlockSpec(band.shape, lambda i, s: (0, 0)),
            pl.BlockSpec(memory_space=pl.ANY),
        ],
        out_specs=pl.BlockSpec((planes, GROUP, flat), lambda i, s: (0, i, 0)),
        scratch_shapes=[
            pltpu.VMEM((2, 3, planes, ROWS, LANES), jnp.bfloat16),
            pltpu.VMEM((planes * span, LANES), jnp.float32),
            pltpu.VMEM((flat // LANES * planes * GROUP, LANES), jnp.float32),
            pltpu.SemaphoreType.DMA((2, 3)),
        ],
    )
    return pl.pallas_call(
        hphi_kernel,
        out_shape=jax.ShapeDtypeStruct((planes, owned, flat), jnp.bfloat16),
        grid_spec=grid_spec,
        compiler_params=pltpu.CompilerParams(vmem_limit_bytes=VMEM),
        name="hphi",
        cost_estimate=pl.CostEstimate(
            flops=4 * planes * owned * flat * COLS, bytes_accessed=30 << 20, transcendentals=0
        ),
    )(info, phi, halo, band, pot)


def dense_rows(cols, blocks, dense):
    def one_block(n, carry):
        i = n // NNZB
        col = cols[i, lax.rem(n, NNZB)]
        dense[pl.ds(pl.multiple_of(i * BLK, BLK), BLK), pl.ds(pl.multiple_of(col * BLK, BLK), BLK)] = (
            blocks[pl.ds(pl.multiple_of(n * BLK, BLK), BLK), :]
        )
        return carry

    lax.fori_loop(0, NB * NNZB, one_block, 0)


def first_kernel(k_cols, h_cols, k_blocks, h_blocks, phi, dense_k, product, dense_h):
    @pl.when(pl.program_id(0) == 0)
    def _():
        dense_rows(k_cols, k_blocks, dense_k)
        dense_rows(h_cols, h_blocks, dense_h)

    kphi = jnp.dot(dense_k[...], phi[...], preferred_element_type=jnp.float32)
    product[...] = jnp.dot(
        dense_h[...], kphi.astype(jnp.bfloat16), preferred_element_type=jnp.float32
    )


def first_products(k_cols, h_cols, k_blocks, h_blocks, phi):
    width = phi.shape[1]
    tile = min(COLS, width)
    whole = pl.BlockSpec(k_blocks.shape, lambda i, a, b: (0, 0), pipeline_mode=pl.Buffered(1))
    grid_spec = pltpu.PrefetchScalarGridSpec(
        num_scalar_prefetch=2,
        grid=(width // tile,),
        in_specs=[whole, whole, pl.BlockSpec((NF, tile), lambda i, a, b: (0, i))],
        out_specs=[
            pl.BlockSpec((NF, NF), lambda i, a, b: (0, 0)),
            pl.BlockSpec((NF, tile), lambda i, a, b: (0, i)),
        ],
        scratch_shapes=[pltpu.VMEM((NF, NF), jnp.bfloat16)],
    )
    return pl.pallas_call(
        first_kernel,
        out_shape=[
            jax.ShapeDtypeStruct((NF, NF), jnp.bfloat16),
            jax.ShapeDtypeStruct((NF, width), jnp.float32),
        ],
        grid_spec=grid_spec,
        compiler_params=pltpu.CompilerParams(vmem_limit_bytes=VMEM),
        name="products",
        cost_estimate=pl.CostEstimate(
            flops=4 * NF * NF * width, bytes_accessed=24 << 20, transcendentals=0
        ),
    )(k_cols, h_cols, k_blocks, h_blocks, phi)


def last_kernel(dense_k, hphi, product, out):
    ydiff = (hphi[...].astype(jnp.float32) - product[...]).astype(jnp.bfloat16)
    out[...] = jnp.dot(dense_k[...], ydiff, preferred_element_type=jnp.float32).astype(jnp.bfloat16)


def last_product(dense_k, hphi, product):
    width = hphi.shape[1]
    tile = min(COLS, width)
    columns = pl.BlockSpec((NF, tile), lambda i: (0, i))
    return pl.pallas_call(
        last_kernel,
        out_shape=jax.ShapeDtypeStruct((NF, width), jnp.bfloat16),
        grid=(width // tile,),
        in_specs=[pl.BlockSpec((NF, NF), lambda i: (0, 0)), columns, columns],
        out_specs=columns,
        compiler_params=pltpu.CompilerParams(vmem_limit_bytes=VMEM),
        name="gradient",
        cost_estimate=pl.CostEstimate(
            flops=2 * NF * NF * width, bytes_accessed=17 << 20, transcendentals=0
        ),
    )(dense_k, hphi, product)


def shards(orbitals, centres, potential, kernel, kernel_cols, hamiltonian, intersection_cols):
    rep = lax.axis_index("rep")
    n_func = lax.axis_size("func")
    n_rep = lax.axis_size("rep")
    owned, planes, flat = orbitals.shape
    z_planes, x_size, y_size = potential.shape
    shares = n_func // planes
    width = flat // shares

    def exchange(rows):
        return lax.all_to_all(rows, "func", split_axis=0, concat_axis=0, tiled=True)

    def to_points(plane_rows):
        cut = plane_rows.reshape(planes, owned, shares, width).transpose(0, 2, 1, 3)
        return exchange(cut.reshape(n_func, owned, width)).reshape(n_func * owned, width)

    half = lax.dynamic_slice_in_dim(potential, rep * (x_size // n_rep), x_size // n_rep, axis=1)
    half = half.astype(jnp.bfloat16).reshape(z_planes, x_size // n_rep // ROWS, ROWS, y_size)
    pot = lax.all_gather(half, ("rep", "func"), axis=0, tiled=True)
    pot = pot.reshape(n_rep, n_func * z_planes, x_size // n_rep // ROWS, ROWS, y_size)

    phi_planes = orbitals.transpose(1, 0, 2)
    edge = jnp.where(rep == 0, phi_planes[planes - 2 :], phi_planes[:2])
    halo = lax.ppermute(edge, "rep", [(0, 1), (1, 0)])
    flag = jnp.full((owned, 1), rep, jnp.int32)
    info = jnp.concatenate(
        [centres[:, :1] + planes * rep, centres[:, 1:], flag], axis=1
    ).astype(jnp.int32)

    phi_pts = to_points(phi_planes)
    k_blocks = lax.all_gather(kernel, ("rep", "func"), axis=1, tiled=True).reshape(-1, BLK)
    h_blocks = lax.all_gather(hamiltonian, ("rep", "func"), axis=1, tiled=True).reshape(-1, BLK)

    extra = -owned % GROUP
    padded = [
        jnp.pad(info, ((0, extra), (0, 0))),
        jnp.pad(phi_planes, ((0, 0), (0, extra), (0, 0))),
        jnp.pad(halo, ((0, 0), (0, extra), (0, 0))),
    ]
    hphi = make_hphi(*padded, planar_band(), pot)[:, :owned]
    dense_k, product = first_products(kernel_cols, intersection_cols, k_blocks, h_blocks, phi_pts)
    hphi_pts = to_points(hphi)
    gradient = last_product(dense_k, hphi_pts, product)
    back = exchange(gradient.reshape(n_func, owned, width))
    back = back.reshape(planes, shares, owned, width).transpose(2, 0, 1, 3)
    return back.reshape(owned, planes, flat)


def solution(mesh):
    placed = (
        P("func", "rep", None),
        P("func", None),
        P("func", None, None),
        P("rep", "func", None),
        P(),
        P("rep", "func", None),
        P(),
    )
    return jax.shard_map(
        shards, mesh=mesh, in_specs=placed, out_specs=P("func", "rep", None), check_vma=False
    )
```

```python
import jax
import jax.numpy as jnp
from jax import lax
from jax.experimental import pallas as pl
from jax.experimental.pallas import tpu as pltpu
from jax.sharding import PartitionSpec as P

BOX = 32
BLK = 128
NNZB = 12
NB = 12
NF = NB * BLK
LANES = 128
ROWS = 16
GROUP = 16
COLS = 256
VMEM = 56 * 1024 * 1024
SLOTS = 8
PIECES = 2

CENTRE = 90.0
NEAR = -16.0
FAR = 1.0
SCALE = 1.0 / 96.0


def planar_band():
    row = lax.broadcasted_iota(jnp.int32, (2 * COLS, COLS), 0) - LANES
    col = lax.broadcasted_iota(jnp.int32, (2 * COLS, COLS), 1)
    across = jnp.abs((row + LANES) // BOX - (col + LANES) // BOX)
    along = jnp.abs((row + LANES) % BOX - (col + LANES) % BOX)
    band = jnp.zeros((2 * COLS, COLS), jnp.float32)
    for one, other in ((across, along), (along, across)):
        band = jnp.where((one == 0) & (other == 1), NEAR, band)
        band = jnp.where((one == 0) & (other == 2), FAR, band)
    band = jnp.where((across == 0) & (along == 0), CENTRE, band)
    return band.astype(jnp.bfloat16)


def hphi_kernel(
    info, phi, halo, band, pot, out, buf, rows, win, sems
):
    planes, group, flat = phi.shape
    step = pl.program_id(0)
    total = pl.num_programs(0) * group
    x_blocks = pot.shape[1]
    span = 3 * ROWS
    flag = info[0, 3].astype(jnp.float32)

    def copies(index, slot):
        z = info[index, 0]
        first = info[index, 1] // ROWS
        out_list = []
        for k in range(3):
            block = lax.rem(first + k, 2 * x_blocks)
            out_list.append(
                pltpu.make_async_copy(
                    pot.at[block // x_blocks, lax.rem(block, x_blocks), pl.ds(z, planes)],
                    buf.at[slot, k],
                    sems.at[slot, k],
                )
            )
        return out_list

    @pl.when(step == 0)
    def _():
        for early in range(SLOTS - 1):
            for copy in copies(early, early):
                copy.start()

    lane = lax.broadcasted_iota(jnp.int32, (8, LANES), 1)

    def one_function(f, carry):
        index = step * group + f
        slot = lax.rem(index, SLOTS)
        ahead = index + SLOTS - 1

        @pl.when(ahead < total)
        def _():
            for copy in copies(ahead, lax.rem(ahead, SLOTS)):
                copy.start()

        for copy in copies(index, slot):
            copy.wait()
        for z in range(planes):
            for k in range(3):
                rows[pl.ds(z * span + k * ROWS, ROWS), :] = buf[slot, k, z].astype(jnp.float32)
        shift_x = lax.rem(info[index, 1], ROWS)
        shift_y = info[index, 2]
        for z in range(planes):
            value = None
            for b in range(4):
                part = rows[pl.ds(z * span + b + shift_x, 8, stride=4), :]
                part = pltpu.roll(part, lax.rem(b * BOX + LANES - shift_y, LANES), axis=1)
                value = part if value is None else jnp.where(lane >= b * BOX, part, value)
            win[pl.ds(z * group + f, 8, stride=planes * group), :] = value
        return carry

    lax.fori_loop(0, group, one_function, 0)

    pieces = flat // COLS
    for c in range(pieces):
        low = max(0, c * COLS - LANES)
        high = min(flat, c * COLS + COLS + LANES)
        cols = slice(c * COLS, (c + 1) * COLS)
        left = phi[:, :, low:high].reshape(planes * group, high - low)
        base = low - (c * COLS - LANES)
        planar = jnp.dot(
            left, band[base : base + high - low, :], preferred_element_type=jnp.float32
        )
        level = [phi[z, :, cols].astype(jnp.float32) for z in range(planes)]
        other = [halo[h, :, cols].astype(jnp.float32) for h in range(2)]
        below = [h * flag for h in other]
        above = [h * (1.0 - flag) for h in other]
        level = below + level + above
        for z in range(planes):
            kin = planar[z * group : (z + 1) * group]
            kin = kin + NEAR * (level[z + 1] + level[z + 3]) + FAR * (level[z] + level[z + 4])
            w = jnp.concatenate(
                [
                    win[pl.ds((a * planes + z) * group, group), :]
                    for a in range(c * COLS // LANES, (c + 1) * COLS // LANES)
                ],
                axis=1,
            )
            vphi = (w * level[z + 2]).astype(jnp.bfloat16).astype(jnp.float32)
            out[z, :, cols] = (SCALE * kin + vphi).astype(jnp.bfloat16)


def make_hphi(info, phi, halo, band, pot):
    planes, owned, flat = phi.shape
    span = 3 * ROWS
    grid_spec = pltpu.PrefetchScalarGridSpec(
        num_scalar_prefetch=1,
        grid=(owned // GROUP,),
        in_specs=[
            pl.BlockSpec((planes, GROUP, flat), lambda i, s: (0, i, 0)),
            pl.BlockSpec((2, GROUP, flat), lambda i, s: (0, i, 0)),
            pl.BlockSpec(band.shape, lambda i, s: (0, 0)),
            pl.BlockSpec(memory_space=pl.ANY),
        ],
        out_specs=pl.BlockSpec((planes, GROUP, flat), lambda i, s: (0, i, 0)),
        scratch_shapes=[
            pltpu.VMEM((SLOTS, 3, planes, ROWS, LANES), jnp.bfloat16),
            pltpu.VMEM((planes * span, LANES), jnp.float32),
            pltpu.VMEM((flat // LANES * planes * GROUP, LANES), jnp.float32),
            pltpu.SemaphoreType.DMA((SLOTS, 3)),
        ],
    )
    return pl.pallas_call(
        hphi_kernel,
        out_shape=jax.ShapeDtypeStruct((planes, owned, flat), jnp.bfloat16),
        grid_spec=grid_spec,
        compiler_params=pltpu.CompilerParams(vmem_limit_bytes=VMEM),
        name="hphi",
        cost_estimate=pl.CostEstimate(
            flops=4 * planes * owned * flat * COLS, bytes_accessed=30 << 20, transcendentals=0
        ),
    )(info, phi, halo, band, pot)


def dense_rows(cols, blocks, dense):
    def one_block(n, carry):
        i = n // NNZB
        col = cols[i, lax.rem(n, NNZB)]
        dense[pl.ds(pl.multiple_of(i * BLK, BLK), BLK), pl.ds(pl.multiple_of(col * BLK, BLK), BLK)] = (
            blocks[pl.ds(pl.multiple_of(n * BLK, BLK), BLK), :]
        )
        return carry

    lax.fori_loop(0, NB * NNZB, one_block, 0)


def first_kernel(k_cols, h_cols, k_blocks, h_blocks, phi, dense_k, product, dense_h):
    @pl.when(pl.program_id(0) == 0)
    def _():
        dense_rows(k_cols, k_blocks, dense_k)
        dense_rows(h_cols, h_blocks, dense_h)

    kphi = jnp.dot(dense_k[...], phi[...], preferred_element_type=jnp.float32)
    product[...] = jnp.dot(
        dense_h[...], kphi.astype(jnp.bfloat16), preferred_element_type=jnp.float32
    )


def first_products(k_cols, h_cols, k_blocks, h_blocks, phi):
    width = phi.shape[1]
    tile = min(COLS, width)
    whole = pl.BlockSpec(k_blocks.shape, lambda i, a, b: (0, 0), pipeline_mode=pl.Buffered(1))
    grid_spec = pltpu.PrefetchScalarGridSpec(
        num_scalar_prefetch=2,
        grid=(width // tile,),
        in_specs=[whole, whole, pl.BlockSpec((NF, tile), lambda i, a, b: (0, i))],
        out_specs=[
            pl.BlockSpec((NF, NF), lambda i, a, b: (0, 0)),
            pl.BlockSpec((NF, tile), lambda i, a, b: (0, i)),
        ],
        scratch_shapes=[pltpu.VMEM((NF, NF), jnp.bfloat16)],
    )
    return pl.pallas_call(
        first_kernel,
        out_shape=[
            jax.ShapeDtypeStruct((NF, NF), jnp.bfloat16),
            jax.ShapeDtypeStruct((NF, width), jnp.float32),
        ],
        grid_spec=grid_spec,
        compiler_params=pltpu.CompilerParams(vmem_limit_bytes=VMEM),
        name="products",
        cost_estimate=pl.CostEstimate(
            flops=4 * NF * NF * width, bytes_accessed=24 << 20, transcendentals=0
        ),
    )(k_cols, h_cols, k_blocks, h_blocks, phi)


def last_kernel(dense_k, hphi, product, out):
    ydiff = (hphi[...].astype(jnp.float32) - product[...]).astype(jnp.bfloat16)
    out[...] = jnp.dot(dense_k[...], ydiff, preferred_element_type=jnp.float32).astype(jnp.bfloat16)


def last_product(dense_k, hphi, product):
    width = hphi.shape[1]
    tile = min(COLS, width)
    columns = pl.BlockSpec((NF, tile), lambda i: (0, i))
    return pl.pallas_call(
        last_kernel,
        out_shape=jax.ShapeDtypeStruct((NF, width), jnp.bfloat16),
        grid=(width // tile,),
        in_specs=[pl.BlockSpec((NF, NF), lambda i: (0, 0)), columns, columns],
        out_specs=columns,
        compiler_params=pltpu.CompilerParams(vmem_limit_bytes=VMEM),
        name="gradient",
        cost_estimate=pl.CostEstimate(
            flops=2 * NF * NF * width, bytes_accessed=17 << 20, transcendentals=0
        ),
    )(dense_k, hphi, product)


SIDES = (4, 2, 2)


def place_of():
    me = lax.axis_index("func")
    return me // 4, (me // 2) % 2, me % 2


def along_z(part):
    z = place_of()[0]
    n = lax.axis_size("func")
    held = [part]
    for k in range(1, 4):
        held.append(lax.ppermute(part, "func", [(i, (i + 4 * k) % n) for i in range(n)]))

    def at(level):
        taken = held[0]
        for k in range(1, 4):
            taken = jnp.where((z - level) % 4 == k, held[k], taken)
        return taken

    return jnp.stack([at(level) for level in range(4)])


def swapped(block, bit):
    n = lax.axis_size("func")
    return lax.ppermute(block, "func", [(i, i ^ bit) for i in range(n)])


def other_core(block):
    return lax.ppermute(block, "rep", [(0, 1), (1, 0)])


def put(whole, piece, blocks, core):
    _, y, x = place_of()
    for block, (to_y, to_x) in zip(blocks, ((y, x), (y, 1 - x), (1 - y, x), (1 - y, 1 - x))):
        rest = whole.ndim - 5
        start = (core, piece, 0, to_y, to_x) + (0,) * rest
        whole = lax.dynamic_update_slice(whole, block, start)
    return whole


def shards(orbitals, centres, potential, kernel, kernel_cols, hamiltonian, intersection_cols):
    rep = lax.axis_index("rep")
    n_func = lax.axis_size("func")
    n_rep = lax.axis_size("rep")
    owned, planes, flat = orbitals.shape
    z_planes, x_size, y_size = potential.shape
    shares = n_func // planes
    width = flat // shares
    x_blocks = x_size // n_rep // ROWS

    def exchange(rows):
        return lax.all_to_all(rows, "func", split_axis=0, concat_axis=0, tiled=True)

    def cut(plane_rows):
        pieces = plane_rows.reshape(planes, owned, shares, width).transpose(0, 2, 1, 3)
        return pieces.reshape(n_func, owned, width)

    half = lax.dynamic_slice_in_dim(potential, rep * (x_size // n_rep), x_size // n_rep, axis=1)
    half = half.astype(jnp.bfloat16).reshape(z_planes, x_blocks, ROWS, y_size).transpose(1, 0, 2, 3)
    phi_planes = orbitals.transpose(1, 0, 2)
    phi_cut = cut(phi_planes)
    edge = jnp.where(rep == 0, phi_planes[planes - 2 :], phi_planes[:2])
    halo = lax.ppermute(edge, "rep", [(0, 1), (1, 0)])
    flag = jnp.full((owned, 1), rep, jnp.int32)
    info = jnp.concatenate(
        [centres[:, :1] + planes * rep, centres[:, 1:], flag], axis=1
    ).astype(jnp.int32)

    if n_func == 16:
        per = x_blocks // PIECES
        lines = [along_z(half[p * per : (p + 1) * per]) for p in range(PIECES)]
        lines, phi_cut = lax.optimization_barrier((lines, phi_cut))
        phi_pts = exchange(phi_cut)
        near = [swapped(lines[p], 1 + p) for p in range(PIECES)]
        far = [(swapped(lines[p], 2 - p), swapped(near[p], 2 - p)) for p in range(PIECES)]
        pot = jnp.zeros((n_rep, x_blocks) + SIDES + (z_planes, ROWS, y_size), jnp.bfloat16)
        for p in range(PIECES):
            blocks = [lines[p], near[p], *far[p]] if p == 0 else [lines[p], far[p][0], near[p], far[p][1]]
            for core, group in ((rep, blocks), (1 - rep, [other_core(b) for b in blocks])):
                laid = [b.transpose(1, 0, 2, 3, 4)[None, :, :, None, None] for b in group]
                pot = put(pot, per * p, laid, core)
        pot = pot.reshape(n_rep, x_blocks, n_func * z_planes, ROWS, y_size)

        near, kernel, hamiltonian = lax.optimization_barrier((near, kernel, hamiltonian))
        gathered = []
        for p, stored in enumerate((kernel, hamiltonian)):
            line = along_z(stored[0])
            close = swapped(line, 1 + p)
            rest = (swapped(line, 2 - p), swapped(close, 2 - p))
            blocks = [line, close, *rest] if p == 0 else [line, rest[0], close, rest[1]]
            whole = jnp.zeros((n_rep, 1) + SIDES + stored.shape[1:], jnp.bfloat16)
            for core, group in ((rep, blocks), (1 - rep, [other_core(b) for b in blocks])):
                whole = put(whole, 0, [b[None, None, :, None, None] for b in group], core)
            gathered.append(whole.reshape(-1, BLK))
        k_blocks, h_blocks = gathered
    else:
        pot = lax.all_gather(half, ("rep", "func"), axis=0, tiled=False)
        pot = pot.reshape(n_rep, n_func, x_blocks, z_planes, ROWS, y_size)
        pot = pot.transpose(0, 2, 1, 3, 4, 5)
        pot = pot.reshape(n_rep, x_blocks, n_func * z_planes, ROWS, y_size)
        phi_pts = exchange(phi_cut)
        k_blocks, h_blocks = (
            lax.all_gather(stored, ("rep", "func"), axis=1, tiled=True).reshape(-1, BLK)
            for stored in (kernel, hamiltonian)
        )

    extra = -owned % GROUP
    padded = [
        jnp.pad(info, ((0, extra), (0, 0))),
        jnp.pad(phi_planes, ((0, 0), (0, extra), (0, 0))),
        jnp.pad(halo, ((0, 0), (0, extra), (0, 0))),
    ]
    hphi = make_hphi(*padded, planar_band(), pot)[:, :owned]
    phi_pts = phi_pts.reshape(n_func * owned, width)
    dense_k, product = first_products(kernel_cols, intersection_cols, k_blocks, h_blocks, phi_pts)
    hphi_pts = exchange(cut(hphi)).reshape(n_func * owned, width)
    gradient = last_product(dense_k, hphi_pts, product)
    back = exchange(gradient.reshape(n_func, owned, width))
    back = back.reshape(planes, shares, owned, width).transpose(2, 0, 1, 3)
    return back.reshape(owned, planes, flat)


def solution(mesh):
    placed = (
        P("func", "rep", None),
        P("func", None),
        P("func", None, None),
        P("rep", "func", None),
        P(),
        P("rep", "func", None),
        P(),
    )
    return jax.shard_map(
        shards, mesh=mesh, in_specs=placed, out_specs=P("func", "rep", None), check_vma=False
    )
```

```python
import functools

import jax
import jax.numpy as jnp
from jax import lax
from jax.experimental import pallas as pl
from jax.experimental.pallas import tpu as pltpu
from jax.sharding import PartitionSpec as P

BOX = 32
BLK = 128
NNZB = 12
NB = 12
NF = NB * BLK
LANES = 128
ROWS = 16
GROUP = 16
COLS = 256
VMEM = 56 * 1024 * 1024
SLOTS = 8
PIECES = 2

CENTRE = 90.0
NEAR = -16.0
FAR = 1.0
SCALE = 1.0 / 96.0


SIDES = (4, 2, 2)


def block_places(here, blocks, pieces=PIECES):
    rep, y, x = (here[k] for k in range(3))
    places = []
    for n, block in enumerate(blocks):
        core = rep if n < len(blocks) // 2 else 1 - rep
        piece = n // 4 % pieces
        to_y = y if n % 4 < 2 else 1 - y
        to_x = x if n % 2 == 0 else 1 - x
        places.append((block, core, piece, to_y * SIDES[2] + to_x))
    return places


def planar_band():
    row = lax.broadcasted_iota(jnp.int32, (2 * COLS, COLS), 0) - LANES
    col = lax.broadcasted_iota(jnp.int32, (2 * COLS, COLS), 1)
    across = jnp.abs((row + LANES) // BOX - (col + LANES) // BOX)
    along = jnp.abs((row + LANES) % BOX - (col + LANES) % BOX)
    band = jnp.zeros((2 * COLS, COLS), jnp.float32)
    for one, other in ((across, along), (along, across)):
        band = jnp.where((one == 0) & (other == 1), NEAR, band)
        band = jnp.where((one == 0) & (other == 2), FAR, band)
    band = jnp.where((across == 0) & (along == 0), CENTRE, band)
    return band.astype(jnp.bfloat16)


def hphi_kernel(info, here, phi, halo, band, *refs, resident):
    planes, group, flat = phi.shape
    step = pl.program_id(0)
    total = pl.num_programs(0) * group
    span = 3 * ROWS
    flag = here[0].astype(jnp.float32)
    if resident:
        blocks, (out, pot, rows, win, sems) = refs[:-5], refs[-5:]
    else:
        pot, out, buf, rows, win, sems = refs
    x_blocks = pot.shape[1]

    def copies(index, slot):
        z = info[index, 0]
        first = info[index, 1] // ROWS
        out_list = []
        for k in range(3):
            block = lax.rem(first + k, 2 * x_blocks)
            out_list.append(
                pltpu.make_async_copy(
                    pot.at[block // x_blocks, lax.rem(block, x_blocks), pl.ds(z, planes)],
                    buf.at[slot, k],
                    sems.at[slot, k],
                )
            )
        return out_list

    @pl.when(step == 0)
    def _():
        if resident:
            started = []
            for n, (block, core, piece, column) in enumerate(block_places(here, blocks)):
                per, depth = block.shape[1:3]
                for z in range(SIDES[0]):
                    target = pl.multiple_of((z * SIDES[1] * SIDES[2] + column) * depth, depth)
                    started.append(
                        pltpu.make_async_copy(
                            block.at[z],
                            pot.at[core, pl.ds(piece * per, per), pl.ds(target, depth)],
                            sems.at[n, z],
                        )
                    )
            for copy in started:
                copy.start()
            for copy in started:
                copy.wait()
        else:
            for early in range(SLOTS - 1):
                for copy in copies(early, early):
                    copy.start()

    lane = lax.broadcasted_iota(jnp.int32, (8, LANES), 1)

    def one_function(f, carry):
        index = step * group + f
        if resident:
            z0 = info[index, 0]
            first = info[index, 1] // ROWS
            for k in range(3):
                block = lax.rem(first + k, 2 * x_blocks)
                source = pot.at[block // x_blocks, lax.rem(block, x_blocks)]
                for z in range(planes):
                    rows[pl.ds(z * span + k * ROWS, ROWS), :] = source[z0 + z].astype(jnp.float32)
        else:
            slot = lax.rem(index, SLOTS)
            ahead = index + SLOTS - 1

            @pl.when(ahead < total)
            def _():
                for copy in copies(ahead, lax.rem(ahead, SLOTS)):
                    copy.start()

            for copy in copies(index, slot):
                copy.wait()
            for z in range(planes):
                for k in range(3):
                    rows[pl.ds(z * span + k * ROWS, ROWS), :] = buf[slot, k, z].astype(jnp.float32)
        shift_x = lax.rem(info[index, 1], ROWS)
        shift_y = info[index, 2]
        for z in range(planes):
            value = None
            for b in range(4):
                part = rows[pl.ds(z * span + b + shift_x, 8, stride=4), :]
                part = pltpu.roll(part, lax.rem(b * BOX + LANES - shift_y, LANES), axis=1)
                value = part if value is None else jnp.where(lane >= b * BOX, part, value)
            win[pl.ds(z * group + f, 8, stride=planes * group), :] = value
        return carry

    lax.fori_loop(0, group, one_function, 0)

    pieces = flat // COLS
    for c in range(pieces):
        low = max(0, c * COLS - LANES)
        high = min(flat, c * COLS + COLS + LANES)
        cols = slice(c * COLS, (c + 1) * COLS)
        left = phi[:, :, low:high].reshape(planes * group, high - low)
        base = low - (c * COLS - LANES)
        planar = jnp.dot(
            left, band[base : base + high - low, :], preferred_element_type=jnp.float32
        )
        level = [phi[z, :, cols].astype(jnp.float32) for z in range(planes)]
        other = [halo[h, :, cols].astype(jnp.float32) for h in range(2)]
        below = [h * flag for h in other]
        above = [h * (1.0 - flag) for h in other]
        level = below + level + above
        for z in range(planes):
            kin = planar[z * group : (z + 1) * group]
            kin = kin + NEAR * (level[z + 1] + level[z + 3]) + FAR * (level[z] + level[z + 4])
            w = jnp.concatenate(
                [
                    win[pl.ds((a * planes + z) * group, group), :]
                    for a in range(c * COLS // LANES, (c + 1) * COLS // LANES)
                ],
                axis=1,
            )
            vphi = (w * level[z + 2]).astype(jnp.bfloat16).astype(jnp.float32)
            out[z, :, cols] = (SCALE * kin + vphi).astype(jnp.bfloat16)


def make_hphi(info, here, phi, halo, band, blocks, resident):
    planes, owned, flat = phi.shape
    span = 3 * ROWS
    if resident:
        per, depth = blocks[0].shape[1:3]
        size = (2, PIECES * per, SIDES[0] * SIDES[1] * SIDES[2] * depth, ROWS, LANES)
        taken = pltpu.VMEM(size, jnp.bfloat16)
        sems = pltpu.SemaphoreType.DMA((len(blocks), SIDES[0]))
    else:
        taken = pltpu.VMEM((SLOTS, 3, planes, ROWS, LANES), jnp.bfloat16)
        sems = pltpu.SemaphoreType.DMA((SLOTS, 3))
    grid_spec = pltpu.PrefetchScalarGridSpec(
        num_scalar_prefetch=2,
        grid=(owned // GROUP,),
        in_specs=[
            pl.BlockSpec((planes, GROUP, flat), lambda i, s, t: (0, i, 0)),
            pl.BlockSpec((2, GROUP, flat), lambda i, s, t: (0, i, 0)),
            pl.BlockSpec(band.shape, lambda i, s, t: (0, 0)),
        ]
        + [pl.BlockSpec(memory_space=pl.ANY)] * len(blocks),
        out_specs=pl.BlockSpec((planes, GROUP, flat), lambda i, s, t: (0, i, 0)),
        scratch_shapes=[
            taken,
            pltpu.VMEM((planes * span, LANES), jnp.float32),
            pltpu.VMEM((flat // LANES * planes * GROUP, LANES), jnp.float32),
            sems,
        ],
    )
    return pl.pallas_call(
        functools.partial(hphi_kernel, resident=resident),
        out_shape=jax.ShapeDtypeStruct((planes, owned, flat), jnp.bfloat16),
        grid_spec=grid_spec,
        compiler_params=pltpu.CompilerParams(vmem_limit_bytes=VMEM),
        name="hphi",
        cost_estimate=pl.CostEstimate(
            flops=8 * planes * owned * flat * flat, bytes_accessed=60 << 20, transcendentals=0
        ),
    )(info, here, phi, halo, band, *blocks)


def dense_rows(cols, blocks, dense):
    def one_block(n, carry):
        i = n // NNZB
        col = cols[i, lax.rem(n, NNZB)]
        dense[pl.ds(pl.multiple_of(i * BLK, BLK), BLK), pl.ds(pl.multiple_of(col * BLK, BLK), BLK)] = (
            blocks[pl.ds(pl.multiple_of(n * BLK, BLK), BLK), :]
        )
        return carry

    lax.fori_loop(0, NB * NNZB, one_block, 0, unroll=4)


def first_kernel(here, k_cols, h_cols, *refs):
    phi, dense_k, product, dense_h, k_blocks, h_blocks, sems = refs[-7:]
    half = (len(refs) - 7) // 2
    depth = refs[0].shape[-2]

    def copies(which):
        stored = refs[which * half : (which + 1) * half]
        target = (k_blocks, h_blocks)[which]
        if half == 1:
            return [pltpu.make_async_copy(stored[0], target, sems.at[which, 0, 0])]
        out_list = []
        columns = SIDES[1] * SIDES[2]
        for n, (block, core, _, column) in enumerate(block_places(here, stored, 1)):
            for z in range(SIDES[0]):
                row = ((core * SIDES[0] + z) * columns + column) * depth
                out_list.append(
                    pltpu.make_async_copy(
                        block.at[z],
                        target.at[pl.ds(pl.multiple_of(row, depth), depth)],
                        sems.at[which, n, z],
                    )
                )
        return out_list

    @pl.when(pl.program_id(0) == 0)
    def _():
        for which in range(2):
            for copy in copies(which):
                copy.start()
        for which, (cols, blocks, dense) in enumerate(
            ((k_cols, k_blocks, dense_k), (h_cols, h_blocks, dense_h))
        ):
            for copy in copies(which):
                copy.wait()
            dense_rows(cols, blocks, dense)

    kphi = jnp.dot(dense_k[...], phi[...], preferred_element_type=jnp.float32)
    product[...] = jnp.dot(
        dense_h[...], kphi.astype(jnp.bfloat16), preferred_element_type=jnp.float32
    )


def first_products(here, k_cols, h_cols, k_parts, h_parts, phi):
    width = phi.shape[1]
    tile = min(COLS, width)
    stored = pltpu.VMEM((NB * NNZB * BLK, BLK), jnp.bfloat16)
    grid_spec = pltpu.PrefetchScalarGridSpec(
        num_scalar_prefetch=3,
        grid=(width // tile,),
        in_specs=[pl.BlockSpec(memory_space=pl.ANY)] * (2 * len(k_parts))
        + [pl.BlockSpec((NF, tile), lambda i, *s: (0, i))],
        out_specs=[
            pl.BlockSpec((NF, NF), lambda i, *s: (0, 0)),
            pl.BlockSpec((NF, tile), lambda i, *s: (0, i)),
        ],
        scratch_shapes=[
            pltpu.VMEM((NF, NF), jnp.bfloat16),
            stored,
            stored,
            pltpu.SemaphoreType.DMA((2, len(k_parts), SIDES[0])),
        ],
    )
    return pl.pallas_call(
        first_kernel,
        out_shape=[
            jax.ShapeDtypeStruct((NF, NF), jnp.bfloat16),
            jax.ShapeDtypeStruct((NF, width), jnp.float32),
        ],
        grid_spec=grid_spec,
        compiler_params=pltpu.CompilerParams(vmem_limit_bytes=VMEM),
        name="products",
        cost_estimate=pl.CostEstimate(
            flops=4 * NF * NF * width, bytes_accessed=24 << 20, transcendentals=0
        ),
    )(here, k_cols, h_cols, *k_parts, *h_parts, phi)


def last_kernel(dense_k, hphi, product, out):
    ydiff = (hphi[...].astype(jnp.float32) - product[...]).astype(jnp.bfloat16)
    out[...] = jnp.dot(dense_k[...], ydiff, preferred_element_type=jnp.float32).astype(jnp.bfloat16)


def last_product(dense_k, hphi, product):
    width = hphi.shape[1]
    tile = min(COLS, width)
    columns = pl.BlockSpec((NF, tile), lambda i: (0, i))
    return pl.pallas_call(
        last_kernel,
        out_shape=jax.ShapeDtypeStruct((NF, width), jnp.bfloat16),
        grid=(width // tile,),
        in_specs=[pl.BlockSpec((NF, NF), lambda i: (0, 0)), columns, columns],
        out_specs=columns,
        compiler_params=pltpu.CompilerParams(vmem_limit_bytes=VMEM),
        name="gradient",
        cost_estimate=pl.CostEstimate(
            flops=2 * NF * NF * width, bytes_accessed=17 << 20, transcendentals=0
        ),
    )(dense_k, hphi, product)


def place_of():
    me = lax.axis_index("func")
    return me // 4, (me // 2) % 2, me % 2


def along_z(part):
    z = place_of()[0]
    n = lax.axis_size("func")
    held = [part]
    for k in range(1, 4):
        held.append(lax.ppermute(part, "func", [(i, (i + 4 * k) % n) for i in range(n)]))

    def at(level):
        taken = held[0]
        for k in range(1, 4):
            taken = jnp.where((z - level) % 4 == k, held[k], taken)
        return taken

    return jnp.stack([at(level) for level in range(4)])


def swapped(block, bit):
    n = lax.axis_size("func")
    return lax.ppermute(block, "func", [(i, i ^ bit) for i in range(n)])


def ordered(lines, near, far, first=0):
    blocks = []
    for p, (line, close, (apart, corner)) in enumerate(zip(lines, near, far)):
        middle = [close, apart] if (p + first) % 2 == 0 else [apart, close]
        blocks += [line, *middle, corner]
    return blocks


def other_core(block):
    return lax.ppermute(block, "rep", [(0, 1), (1, 0)])


def shards(orbitals, centres, potential, kernel, kernel_cols, hamiltonian, intersection_cols):
    rep = lax.axis_index("rep")
    n_func = lax.axis_size("func")
    n_rep = lax.axis_size("rep")
    owned, planes, flat = orbitals.shape
    z_planes, x_size, y_size = potential.shape
    shares = n_func // planes
    width = flat // shares
    x_blocks = x_size // n_rep // ROWS

    def exchange(rows):
        return lax.all_to_all(rows, "func", split_axis=0, concat_axis=0, tiled=True)

    def cut(plane_rows):
        pieces = plane_rows.reshape(planes, owned, shares, width).transpose(0, 2, 1, 3)
        return pieces.reshape(n_func, owned, width)

    half = lax.dynamic_slice_in_dim(potential, rep * (x_size // n_rep), x_size // n_rep, axis=1)
    half = half.astype(jnp.bfloat16).reshape(z_planes, x_blocks, ROWS, y_size).transpose(1, 0, 2, 3)
    phi_planes = orbitals.transpose(1, 0, 2)
    phi_cut = cut(phi_planes)
    edge = jnp.where(rep == 0, phi_planes[planes - 2 :], phi_planes[:2])
    halo = lax.ppermute(edge, "rep", [(0, 1), (1, 0)])
    info = jnp.concatenate([centres[:, :1] + planes * rep, centres[:, 1:]], axis=1)
    info = info.astype(jnp.int32)

    resident = n_func == SIDES[0] * SIDES[1] * SIDES[2]
    if resident:
        _, y, x = place_of()
        here = jnp.stack([rep, y, x]).astype(jnp.int32)
        per = x_blocks // PIECES
        lines = [along_z(half[p * per : (p + 1) * per]) for p in range(PIECES)]
        lines, kernel, hamiltonian = lax.optimization_barrier((lines, kernel, hamiltonian))
        near = [swapped(lines[p], 1 + p) for p in range(PIECES)]
        matrix_lines = [along_z(stored[0]) for stored in (kernel, hamiltonian)]
        far = [(swapped(lines[p], 2 - p), swapped(near[p], 2 - p)) for p in range(PIECES)]
        pot = ordered(lines, near, far)
        pot, matrix_lines, phi_cut = lax.optimization_barrier((pot, matrix_lines, phi_cut))
        pot = pot + [other_core(block) for block in pot]
        phi_pts = exchange(phi_cut)
        matrix_near = [swapped(matrix_lines[p], 1 + p) for p in range(2)]
    else:
        here = jnp.stack([rep, rep, rep]).astype(jnp.int32)
        pot = lax.all_gather(half, ("rep", "func"), axis=0, tiled=False)
        pot = pot.reshape(n_rep, n_func, x_blocks, z_planes, ROWS, y_size)
        pot = pot.transpose(0, 2, 1, 3, 4, 5)
        pot = [pot.reshape(n_rep, x_blocks, n_func * z_planes, ROWS, y_size)]
        phi_pts = exchange(phi_cut)
        k_parts, h_parts = (
            [lax.all_gather(stored, ("rep", "func"), axis=1, tiled=True).reshape(-1, BLK)]
            for stored in (kernel, hamiltonian)
        )

    extra = -owned % GROUP
    padded = [
        jnp.pad(info, ((0, extra), (0, 0))),
        jnp.pad(phi_planes, ((0, 0), (0, extra), (0, 0))),
        jnp.pad(halo, ((0, 0), (0, extra), (0, 0))),
    ]
    info, phi_planes, halo = padded
    hphi = make_hphi(info, here, phi_planes, halo, planar_band(), pot, resident)[:, :owned]
    if resident:
        hphi, matrix_near = lax.optimization_barrier((hphi, matrix_near))
        matrix_far = [
            (swapped(matrix_lines[p], 2 - p), swapped(matrix_near[p], 2 - p)) for p in range(2)
        ]
        k_parts, h_parts = (
            ordered(matrix_lines[p : p + 1], matrix_near[p : p + 1], matrix_far[p : p + 1], p)
            for p in range(2)
        )
        k_parts = k_parts + [other_core(block) for block in k_parts]
        h_parts = h_parts + [other_core(block) for block in h_parts]
    phi_pts = phi_pts.reshape(n_func * owned, width)
    dense_k, product = first_products(
        here, kernel_cols, intersection_cols, k_parts, h_parts, phi_pts
    )
    hphi_pts = exchange(cut(hphi)).reshape(n_func * owned, width)
    gradient = last_product(dense_k, hphi_pts, product)
    back = exchange(gradient.reshape(n_func, owned, width))
    back = back.reshape(planes, shares, owned, width).transpose(2, 0, 1, 3)
    return back.reshape(owned, planes, flat)


def solution(mesh):
    placed = (
        P("func", "rep", None),
        P("func", None),
        P("func", None, None),
        P("rep", "func", None),
        P(),
        P("rep", "func", None),
        P(),
    )
    return jax.shard_map(
        shards, mesh=mesh, in_specs=placed, out_specs=P("func", "rep", None), check_vma=False
    )
```

```python
import functools

import jax
import jax.numpy as jnp
from jax import lax
from jax.experimental import pallas as pl
from jax.experimental.pallas import tpu as pltpu
from jax.sharding import PartitionSpec as P

BOX = 32
BLK = 128
NNZB = 12
NB = 12
NF = NB * BLK
LANES = 128
ROWS = 16
GROUP = 16
COLS = 256
VMEM = 56 * 1024 * 1024
SLOTS = 8
PIECES = 2

CENTRE = 90.0
NEAR = -16.0
FAR = 1.0
SCALE = 1.0 / 96.0


SIDES = (4, 2, 2)


def block_places(here, blocks):
    rep, y, x = (here[k] for k in range(3))
    places = []
    for n, block in enumerate(blocks):
        core = rep if n < len(blocks) // 2 else 1 - rep
        piece = n // 4 % PIECES
        to_y = y if n % 4 < 2 else 1 - y
        to_x = x if n % 2 == 0 else 1 - x
        places.append((block, core, piece, to_y * SIDES[2] + to_x))
    return places


def planar_band():
    row = lax.broadcasted_iota(jnp.int32, (2 * COLS, COLS), 0) - LANES
    col = lax.broadcasted_iota(jnp.int32, (2 * COLS, COLS), 1)
    across = jnp.abs((row + LANES) // BOX - (col + LANES) // BOX)
    along = jnp.abs((row + LANES) % BOX - (col + LANES) % BOX)
    band = jnp.zeros((2 * COLS, COLS), jnp.float32)
    for one, other in ((across, along), (along, across)):
        band = jnp.where((one == 0) & (other == 1), NEAR, band)
        band = jnp.where((one == 0) & (other == 2), FAR, band)
    band = jnp.where((across == 0) & (along == 0), CENTRE, band)
    return band.astype(jnp.bfloat16)


def hphi_kernel(info, here, phi, halo, band, *refs, resident):
    planes, group, flat = phi.shape
    step = pl.program_id(0)
    total = pl.num_programs(0) * group
    span = 3 * ROWS
    flag = here[0].astype(jnp.float32)
    if resident:
        blocks, (out, pot, rows, win, sems) = refs[:-5], refs[-5:]
    else:
        pot, out, buf, rows, win, sems = refs
    x_blocks = pot.shape[1]

    def copies(index, slot):
        z = info[index, 0]
        first = info[index, 1] // ROWS
        out_list = []
        for k in range(3):
            block = lax.rem(first + k, 2 * x_blocks)
            out_list.append(
                pltpu.make_async_copy(
                    pot.at[block // x_blocks, lax.rem(block, x_blocks), pl.ds(z, planes)],
                    buf.at[slot, k],
                    sems.at[slot, k],
                )
            )
        return out_list

    @pl.when(step == 0)
    def _():
        if resident:
            started = []
            for n, (block, core, piece, column) in enumerate(block_places(here, blocks)):
                per, depth = block.shape[1:3]
                for z in range(SIDES[0]):
                    target = pl.multiple_of((z * SIDES[1] * SIDES[2] + column) * depth, depth)
                    started.append(
                        pltpu.make_async_copy(
                            block.at[z],
                            pot.at[core, pl.ds(piece * per, per), pl.ds(target, depth)],
                            sems.at[n, z],
                        )
                    )
            for copy in started:
                copy.start()
            for copy in started:
                copy.wait()
        else:
            for early in range(SLOTS - 1):
                for copy in copies(early, early):
                    copy.start()

    lane = lax.broadcasted_iota(jnp.int32, (8, LANES), 1)

    def one_function(f, carry):
        index = step * group + f
        if resident:
            z0 = info[index, 0]
            first = info[index, 1] // ROWS
            for k in range(3):
                block = lax.rem(first + k, 2 * x_blocks)
                source = pot.at[block // x_blocks, lax.rem(block, x_blocks)]
                for z in range(planes):
                    rows[pl.ds(z * span + k * ROWS, ROWS), :] = source[z0 + z].astype(jnp.float32)
        else:
            slot = lax.rem(index, SLOTS)
            ahead = index + SLOTS - 1

            @pl.when(ahead < total)
            def _():
                for copy in copies(ahead, lax.rem(ahead, SLOTS)):
                    copy.start()

            for copy in copies(index, slot):
                copy.wait()
            for z in range(planes):
                for k in range(3):
                    rows[pl.ds(z * span + k * ROWS, ROWS), :] = buf[slot, k, z].astype(jnp.float32)
        shift_x = lax.rem(info[index, 1], ROWS)
        shift_y = info[index, 2]
        for z in range(planes):
            value = None
            for b in range(4):
                part = rows[pl.ds(z * span + b + shift_x, 8, stride=4), :]
                part = pltpu.roll(part, lax.rem(b * BOX + LANES - shift_y, LANES), axis=1)
                value = part if value is None else jnp.where(lane >= b * BOX, part, value)
            win[pl.ds(z * group + f, 8, stride=planes * group), :] = value
        return carry

    lax.fori_loop(0, group, one_function, 0)

    pieces = flat // COLS
    for c in range(pieces):
        low = max(0, c * COLS - LANES)
        high = min(flat, c * COLS + COLS + LANES)
        cols = slice(c * COLS, (c + 1) * COLS)
        left = phi[:, :, low:high].reshape(planes * group, high - low)
        base = low - (c * COLS - LANES)
        planar = jnp.dot(
            left, band[base : base + high - low, :], preferred_element_type=jnp.float32
        )
        level = [phi[z, :, cols].astype(jnp.float32) for z in range(planes)]
        other = [halo[h, :, cols].astype(jnp.float32) for h in range(2)]
        below = [h * flag for h in other]
        above = [h * (1.0 - flag) for h in other]
        level = below + level + above
        for z in range(planes):
            kin = planar[z * group : (z + 1) * group]
            kin = kin + NEAR * (level[z + 1] + level[z + 3]) + FAR * (level[z] + level[z + 4])
            w = jnp.concatenate(
                [
                    win[pl.ds((a * planes + z) * group, group), :]
                    for a in range(c * COLS // LANES, (c + 1) * COLS // LANES)
                ],
                axis=1,
            )
            vphi = (w * level[z + 2]).astype(jnp.bfloat16).astype(jnp.float32)
            out[z, :, cols] = (SCALE * kin + vphi).astype(jnp.bfloat16)


def make_hphi(info, here, phi, halo, band, blocks, resident):
    planes, owned, flat = phi.shape
    span = 3 * ROWS
    if resident:
        per, depth = blocks[0].shape[1:3]
        size = (2, PIECES * per, SIDES[0] * SIDES[1] * SIDES[2] * depth, ROWS, LANES)
        taken = pltpu.VMEM(size, jnp.bfloat16)
        sems = pltpu.SemaphoreType.DMA((len(blocks), SIDES[0]))
    else:
        taken = pltpu.VMEM((SLOTS, 3, planes, ROWS, LANES), jnp.bfloat16)
        sems = pltpu.SemaphoreType.DMA((SLOTS, 3))
    grid_spec = pltpu.PrefetchScalarGridSpec(
        num_scalar_prefetch=2,
        grid=(owned // GROUP,),
        in_specs=[
            pl.BlockSpec((planes, GROUP, flat), lambda i, s, t: (0, i, 0)),
            pl.BlockSpec((2, GROUP, flat), lambda i, s, t: (0, i, 0)),
            pl.BlockSpec(band.shape, lambda i, s, t: (0, 0)),
        ]
        + [pl.BlockSpec(memory_space=pl.ANY)] * len(blocks),
        out_specs=pl.BlockSpec((planes, GROUP, flat), lambda i, s, t: (0, i, 0)),
        scratch_shapes=[
            taken,
            pltpu.VMEM((planes * span, LANES), jnp.float32),
            pltpu.VMEM((flat // LANES * planes * GROUP, LANES), jnp.float32),
            sems,
        ],
    )
    return pl.pallas_call(
        functools.partial(hphi_kernel, resident=resident),
        out_shape=jax.ShapeDtypeStruct((planes, owned, flat), jnp.bfloat16),
        grid_spec=grid_spec,
        compiler_params=pltpu.CompilerParams(vmem_limit_bytes=VMEM),
        name="hphi",
        cost_estimate=pl.CostEstimate(
            flops=8 * planes * owned * flat * flat, bytes_accessed=60 << 20, transcendentals=0
        ),
    )(info, here, phi, halo, band, *blocks)


def dense_rows(cols, blocks, dense):
    def one_block(n, carry):
        i = n // NNZB
        col = cols[i, lax.rem(n, NNZB)]
        dense[pl.ds(pl.multiple_of(i * BLK, BLK), BLK), pl.ds(pl.multiple_of(col * BLK, BLK), BLK)] = (
            blocks[pl.ds(pl.multiple_of(n * BLK, BLK), BLK), :]
        )
        return carry

    lax.fori_loop(0, NB * NNZB, one_block, 0, unroll=4)


def first_kernel(here, k_cols, h_cols, *refs, resident):
    phi, dense_k, product, dense_h, k_blocks, h_blocks, sems = refs[-7:]
    parts = refs[:-7]

    def copies(which):
        target = (k_blocks, h_blocks)[which]
        if not resident:
            return [pltpu.make_async_copy(parts[which], target, sems.at[which, 0, 0])]
        depth = parts[0].shape[-2]
        rep, y, x, z = (here[k] for k in range(4))
        out_list = []
        for n, part in enumerate(parts):
            core = rep if n < SIDES[0] else 1 - rep
            level = lax.rem(z + SIDES[0] - n % SIDES[0], SIDES[0])
            for c in range(SIDES[1] * SIDES[2]):
                to_y = y if c < 2 else 1 - y
                to_x = x if c % 2 == 0 else 1 - x
                row = (((core * SIDES[0] + level) * SIDES[1] + to_y) * SIDES[2] + to_x) * depth
                out_list.append(
                    pltpu.make_async_copy(
                        part.at[which, c],
                        target.at[pl.ds(pl.multiple_of(row, depth), depth)],
                        sems.at[which, n, c],
                    )
                )
        return out_list

    @pl.when(pl.program_id(0) == 0)
    def _():
        for which in range(2):
            for copy in copies(which):
                copy.start()
        for which, (cols, blocks, dense) in enumerate(
            ((k_cols, k_blocks, dense_k), (h_cols, h_blocks, dense_h))
        ):
            for copy in copies(which):
                copy.wait()
            dense_rows(cols, blocks, dense)

    kphi = jnp.dot(dense_k[...], phi[...], preferred_element_type=jnp.float32)
    product[...] = jnp.dot(
        dense_h[...], kphi.astype(jnp.bfloat16), preferred_element_type=jnp.float32
    )


def first_products(here, k_cols, h_cols, parts, phi, resident):
    width = phi.shape[1]
    tile = min(COLS, width)
    stored = pltpu.VMEM((NB * NNZB * BLK, BLK), jnp.bfloat16)
    grid_spec = pltpu.PrefetchScalarGridSpec(
        num_scalar_prefetch=3,
        grid=(width // tile,),
        in_specs=[pl.BlockSpec(memory_space=pl.ANY)] * len(parts)
        + [pl.BlockSpec((NF, tile), lambda i, *s: (0, i))],
        out_specs=[
            pl.BlockSpec((NF, NF), lambda i, *s: (0, 0)),
            pl.BlockSpec((NF, tile), lambda i, *s: (0, i)),
        ],
        scratch_shapes=[
            pltpu.VMEM((NF, NF), jnp.bfloat16),
            stored,
            stored,
            pltpu.SemaphoreType.DMA((2, len(parts), SIDES[1] * SIDES[2])),
        ],
    )
    return pl.pallas_call(
        functools.partial(first_kernel, resident=resident),
        out_shape=[
            jax.ShapeDtypeStruct((NF, NF), jnp.bfloat16),
            jax.ShapeDtypeStruct((NF, width), jnp.float32),
        ],
        grid_spec=grid_spec,
        compiler_params=pltpu.CompilerParams(vmem_limit_bytes=VMEM),
        name="products",
        cost_estimate=pl.CostEstimate(
            flops=4 * NF * NF * width, bytes_accessed=24 << 20, transcendentals=0
        ),
    )(here, k_cols, h_cols, *parts, phi)


def last_kernel(dense_k, hphi, product, out):
    ydiff = (hphi[...].astype(jnp.float32) - product[...]).astype(jnp.bfloat16)
    out[...] = jnp.dot(dense_k[...], ydiff, preferred_element_type=jnp.float32).astype(jnp.bfloat16)


def last_product(dense_k, hphi, product):
    width = hphi.shape[1]
    tile = min(COLS, width)
    columns = pl.BlockSpec((NF, tile), lambda i: (0, i))
    return pl.pallas_call(
        last_kernel,
        out_shape=jax.ShapeDtypeStruct((NF, width), jnp.bfloat16),
        grid=(width // tile,),
        in_specs=[pl.BlockSpec((NF, NF), lambda i: (0, 0)), columns, columns],
        out_specs=columns,
        compiler_params=pltpu.CompilerParams(vmem_limit_bytes=VMEM),
        name="gradient",
        cost_estimate=pl.CostEstimate(
            flops=2 * NF * NF * width, bytes_accessed=17 << 20, transcendentals=0
        ),
    )(dense_k, hphi, product)


def place_of():
    me = lax.axis_index("func")
    return me // 4, (me // 2) % 2, me % 2


def along_z(part):
    z = place_of()[0]
    n = lax.axis_size("func")
    held = [part]
    for k in range(1, 4):
        held.append(lax.ppermute(part, "func", [(i, (i + 4 * k) % n) for i in range(n)]))

    def at(level):
        taken = held[0]
        for k in range(1, 4):
            taken = jnp.where((z - level) % 4 == k, held[k], taken)
        return taken

    return jnp.stack([at(level) for level in range(4)])


def swapped(block, bit):
    n = lax.axis_size("func")
    return lax.ppermute(block, "func", [(i, i ^ bit) for i in range(n)])


def onward(block, step, up):
    n = lax.axis_size("func")
    plane = n // SIDES[0]
    if up:
        route = [(i, i + plane) for i in range(plane * (step - 1), n - plane)]
    else:
        route = [(i, i - plane) for i in range(plane, n - plane * (step - 1))]
    return lax.ppermute(block, "func", route)


def ordered(lines, near, far):
    blocks = []
    for p, (line, close, (apart, corner)) in enumerate(zip(lines, near, far)):
        middle = [close, apart] if p % 2 == 0 else [apart, close]
        blocks += [line, *middle, corner]
    return blocks


def other_core(block):
    return lax.ppermute(block, "rep", [(0, 1), (1, 0)])


def shards(orbitals, centres, potential, kernel, kernel_cols, hamiltonian, intersection_cols):
    rep = lax.axis_index("rep")
    n_func = lax.axis_size("func")
    n_rep = lax.axis_size("rep")
    owned, planes, flat = orbitals.shape
    z_planes, x_size, y_size = potential.shape
    shares = n_func // planes
    width = flat // shares
    x_blocks = x_size // n_rep // ROWS

    def exchange(rows):
        return lax.all_to_all(rows, "func", split_axis=0, concat_axis=0, tiled=True)

    def cut(plane_rows):
        pieces = plane_rows.reshape(planes, owned, shares, width).transpose(0, 2, 1, 3)
        return pieces.reshape(n_func, owned, width)

    half = lax.dynamic_slice_in_dim(potential, rep * (x_size // n_rep), x_size // n_rep, axis=1)
    half = half.astype(jnp.bfloat16).reshape(z_planes, x_blocks, ROWS, y_size).transpose(1, 0, 2, 3)
    phi_planes = orbitals.transpose(1, 0, 2)
    phi_cut = cut(phi_planes)
    edge = jnp.where(rep == 0, phi_planes[planes - 2 :], phi_planes[:2])
    halo = lax.ppermute(edge, "rep", [(0, 1), (1, 0)])
    info = jnp.concatenate([centres[:, :1] + planes * rep, centres[:, 1:]], axis=1)
    info = info.astype(jnp.int32)
    band = planar_band()

    resident = n_func == SIDES[0] * SIDES[1] * SIDES[2]
    if resident:
        level, y, x = place_of()
        here = jnp.stack([rep, y, x, level]).astype(jnp.int32)
        per = x_blocks // PIECES
        stored = [kernel[0], hamiltonian[0]]
        lines = [along_z(half[p * per : (p + 1) * per]) for p in range(PIECES)]
        close = [swapped(stored[p], 1 + p) for p in range(2)]
        apart = [(swapped(stored[p], 2 - p), swapped(close[p], 2 - p)) for p in range(2)]
        around = ordered(stored, close, apart)
        around = jnp.stack([jnp.stack(around[:4]), jnp.stack(around[4:])])
        lines, around, halo, band, info, phi_cut = lax.optimization_barrier(
            (lines, around, halo, band, info, phi_cut)
        )
        near = [swapped(lines[p], 1 + p) for p in range(PIECES)]
        ups, downs = [onward(around, 1, True)], [onward(around, 1, False)]
        lines_too = [other_core(block) for block in lines]
        near, ups, downs = lax.optimization_barrier((near, ups, downs))
        far = [(swapped(lines[p], 2 - p), swapped(near[p], 2 - p)) for p in range(PIECES)]
        ups.append(onward(ups[0], 2, True))
        downs.append(onward(downs[0], 2, False))
        near_too = [other_core(block) for block in near]
        far, ups, downs, phi_cut, lines_too, near_too = lax.optimization_barrier(
            (far, ups, downs, phi_cut, lines_too, near_too)
        )
        phi_pts = exchange(phi_cut)
        ups.append(onward(ups[1], 3, True))
        downs.append(onward(downs[1], 3, False))
        far_too = [tuple(other_core(block) for block in pair) for pair in far]
        pot = ordered(lines, near, far) + ordered(lines_too, near_too, far_too)
    else:
        here = jnp.stack([rep, rep, rep, rep]).astype(jnp.int32)
        pot = lax.all_gather(half, ("rep", "func"), axis=0, tiled=False)
        pot = pot.reshape(n_rep, n_func, x_blocks, z_planes, ROWS, y_size)
        pot = pot.transpose(0, 2, 1, 3, 4, 5)
        pot = [pot.reshape(n_rep, x_blocks, n_func * z_planes, ROWS, y_size)]
        phi_pts = exchange(phi_cut)
        parts = [
            lax.all_gather(stored, ("rep", "func"), axis=1, tiled=True).reshape(-1, BLK)
            for stored in (kernel, hamiltonian)
        ]

    extra = -owned % GROUP
    padded = [
        jnp.pad(info, ((0, extra), (0, 0))),
        jnp.pad(phi_planes, ((0, 0), (0, extra), (0, 0))),
        jnp.pad(halo, ((0, 0), (0, extra), (0, 0))),
    ]
    info, phi_planes, halo = padded
    hphi = make_hphi(info, here, phi_planes, halo, band, pot, resident)[:, :owned]
    if resident:
        hphi, ups, downs = lax.optimization_barrier((hphi, ups, downs))
        parts = [around]
        for k in range(1, SIDES[0]):
            parts.append(jnp.where(level >= k, ups[k - 1], downs[SIDES[0] - 1 - k]))
        parts = parts + [other_core(part) for part in parts]
    phi_pts = phi_pts.reshape(n_func * owned, width)
    dense_k, product = first_products(
        here, kernel_cols, intersection_cols, parts, phi_pts, resident
    )
    hphi_pts = exchange(cut(hphi)).reshape(n_func * owned, width)
    gradient = last_product(dense_k, hphi_pts, product)
    back = exchange(gradient.reshape(n_func, owned, width))
    back = back.reshape(planes, shares, owned, width).transpose(2, 0, 1, 3)
    return back.reshape(owned, planes, flat)


def solution(mesh):
    placed = (
        P("func", "rep", None),
        P("func", None),
        P("func", None, None),
        P("rep", "func", None),
        P(),
        P("rep", "func", None),
        P(),
    )
    return jax.shard_map(
        shards, mesh=mesh, in_specs=placed, out_specs=P("func", "rep", None), check_vma=False
    )
```

```python
import functools

import jax
import jax.numpy as jnp
from jax import lax
from jax.experimental import pallas as pl
from jax.experimental.pallas import tpu as pltpu
from jax.sharding import PartitionSpec as P

BOX = 32
BLK = 128
NNZB = 12
NB = 12
NF = NB * BLK
LANES = 128
ROWS = 16
GROUP = 16
COLS = 256
VMEM = 56 * 1024 * 1024
SLOTS = 8
PIECES = 2

CENTRE = 90.0
NEAR = -16.0
FAR = 1.0
SCALE = 1.0 / 96.0


SIDES = (4, 2, 2)


def block_places(here, blocks):
    rep, y, x = (here[k] for k in range(3))
    places = []
    for n, block in enumerate(blocks):
        core = rep if n < len(blocks) // 2 else 1 - rep
        piece = n // 4 % PIECES
        to_y = y if n % 4 < 2 else 1 - y
        to_x = x if n % 2 == 0 else 1 - x
        places.append((block, core, piece, to_y * SIDES[2] + to_x))
    return places


def planar_band():
    row = lax.broadcasted_iota(jnp.int32, (2 * COLS, COLS), 0) - LANES
    col = lax.broadcasted_iota(jnp.int32, (2 * COLS, COLS), 1)
    across = jnp.abs((row + LANES) // BOX - (col + LANES) // BOX)
    along = jnp.abs((row + LANES) % BOX - (col + LANES) % BOX)
    band = jnp.zeros((2 * COLS, COLS), jnp.float32)
    for one, other in ((across, along), (along, across)):
        band = jnp.where((one == 0) & (other == 1), NEAR, band)
        band = jnp.where((one == 0) & (other == 2), FAR, band)
    band = jnp.where((across == 0) & (along == 0), CENTRE, band)
    return band.astype(jnp.bfloat16)


def hphi_kernel(info, here, phi, halo, band, *refs, resident):
    planes, group, flat = phi.shape
    step = pl.program_id(0)
    total = pl.num_programs(0) * group
    span = 3 * ROWS
    flag = here[0].astype(jnp.float32)
    if resident:
        blocks, (out, pot, rows, win, sems) = refs[:-5], refs[-5:]
    else:
        pot, out, buf, rows, win, sems = refs
    x_blocks = pot.shape[1]

    def copies(index, slot):
        z = info[index, 0]
        first = info[index, 1] // ROWS
        out_list = []
        for k in range(3):
            block = lax.rem(first + k, 2 * x_blocks)
            out_list.append(
                pltpu.make_async_copy(
                    pot.at[block // x_blocks, lax.rem(block, x_blocks), pl.ds(z, planes)],
                    buf.at[slot, k],
                    sems.at[slot, k],
                )
            )
        return out_list

    @pl.when(step == 0)
    def _():
        if resident:
            started = []
            for n, (block, core, piece, column) in enumerate(block_places(here, blocks)):
                per, depth = block.shape[1:3]
                for z in range(SIDES[0]):
                    target = pl.multiple_of((z * SIDES[1] * SIDES[2] + column) * depth, depth)
                    started.append(
                        pltpu.make_async_copy(
                            block.at[z],
                            pot.at[core, pl.ds(piece * per, per), pl.ds(target, depth)],
                            sems.at[n, z],
                        )
                    )
            for copy in started:
                copy.start()
            for copy in started:
                copy.wait()
        else:
            for early in range(SLOTS - 1):
                for copy in copies(early, early):
                    copy.start()

    lane = lax.broadcasted_iota(jnp.int32, (8, LANES), 1)

    def one_function(f, carry):
        index = step * group + f
        if resident:
            z0 = info[index, 0]
            first = info[index, 1] // ROWS
            for k in range(3):
                block = lax.rem(first + k, 2 * x_blocks)
                source = pot.at[block // x_blocks, lax.rem(block, x_blocks)]
                for z in range(planes):
                    rows[pl.ds(z * span + k * ROWS, ROWS), :] = source[z0 + z].astype(jnp.float32)
        else:
            slot = lax.rem(index, SLOTS)
            ahead = index + SLOTS - 1

            @pl.when(ahead < total)
            def _():
                for copy in copies(ahead, lax.rem(ahead, SLOTS)):
                    copy.start()

            for copy in copies(index, slot):
                copy.wait()
            for z in range(planes):
                for k in range(3):
                    rows[pl.ds(z * span + k * ROWS, ROWS), :] = buf[slot, k, z].astype(jnp.float32)
        shift_x = lax.rem(info[index, 1], ROWS)
        shift_y = info[index, 2]
        for z in range(planes):
            value = None
            for b in range(4):
                part = rows[pl.ds(z * span + b + shift_x, 8, stride=4), :]
                part = pltpu.roll(part, lax.rem(b * BOX + LANES - shift_y, LANES), axis=1)
                value = part if value is None else jnp.where(lane >= b * BOX, part, value)
            win[pl.ds(z * group + f, 8, stride=planes * group), :] = value
        return carry

    lax.fori_loop(0, group, one_function, 0)

    pieces = flat // COLS
    for c in range(pieces):
        low = max(0, c * COLS - LANES)
        high = min(flat, c * COLS + COLS + LANES)
        cols = slice(c * COLS, (c + 1) * COLS)
        left = phi[:, :, low:high].reshape(planes * group, high - low)
        base = low - (c * COLS - LANES)
        planar = jnp.dot(
            left, band[base : base + high - low, :], preferred_element_type=jnp.float32
        )
        level = [phi[z, :, cols].astype(jnp.float32) for z in range(planes)]
        other = [halo[h, :, cols].astype(jnp.float32) for h in range(2)]
        below = [h * flag for h in other]
        above = [h * (1.0 - flag) for h in other]
        level = below + level + above
        for z in range(planes):
            kin = planar[z * group : (z + 1) * group]
            kin = kin + NEAR * (level[z + 1] + level[z + 3]) + FAR * (level[z] + level[z + 4])
            w = jnp.concatenate(
                [
                    win[pl.ds((a * planes + z) * group, group), :]
                    for a in range(c * COLS // LANES, (c + 1) * COLS // LANES)
                ],
                axis=1,
            )
            vphi = (w * level[z + 2]).astype(jnp.bfloat16).astype(jnp.float32)
            out[z, :, cols] = (SCALE * kin + vphi).astype(jnp.bfloat16)


def make_hphi(info, here, phi, halo, band, blocks, resident):
    planes, owned, flat = phi.shape
    span = 3 * ROWS
    if resident:
        per, depth = blocks[0].shape[1:3]
        size = (2, PIECES * per, SIDES[0] * SIDES[1] * SIDES[2] * depth, ROWS, LANES)
        taken = pltpu.VMEM(size, jnp.bfloat16)
        sems = pltpu.SemaphoreType.DMA((len(blocks), SIDES[0]))
    else:
        taken = pltpu.VMEM((SLOTS, 3, planes, ROWS, LANES), jnp.bfloat16)
        sems = pltpu.SemaphoreType.DMA((SLOTS, 3))
    grid_spec = pltpu.PrefetchScalarGridSpec(
        num_scalar_prefetch=2,
        grid=(owned // GROUP,),
        in_specs=[
            pl.BlockSpec((planes, GROUP, flat), lambda i, s, t: (0, i, 0)),
            pl.BlockSpec((2, GROUP, flat), lambda i, s, t: (0, i, 0)),
            pl.BlockSpec(band.shape, lambda i, s, t: (0, 0)),
        ]
        + [pl.BlockSpec(memory_space=pl.ANY)] * len(blocks),
        out_specs=pl.BlockSpec((planes, GROUP, flat), lambda i, s, t: (0, i, 0)),
        scratch_shapes=[
            taken,
            pltpu.VMEM((planes * span, LANES), jnp.float32),
            pltpu.VMEM((flat // LANES * planes * GROUP, LANES), jnp.float32),
            sems,
        ],
    )
    return pl.pallas_call(
        functools.partial(hphi_kernel, resident=resident),
        out_shape=jax.ShapeDtypeStruct((planes, owned, flat), jnp.bfloat16),
        grid_spec=grid_spec,
        compiler_params=pltpu.CompilerParams(vmem_limit_bytes=VMEM),
        name="hphi",
        cost_estimate=pl.CostEstimate(
            flops=8 * planes * owned * flat * flat, bytes_accessed=60 << 20, transcendentals=0
        ),
    )(info, here, phi, halo, band, *blocks)


def dense_rows(cols, blocks, dense):
    def one_block(n, carry):
        i = n // NNZB
        col = cols[i, lax.rem(n, NNZB)]
        dense[pl.ds(pl.multiple_of(i * BLK, BLK), BLK), pl.ds(pl.multiple_of(col * BLK, BLK), BLK)] = (
            blocks[pl.ds(pl.multiple_of(n * BLK, BLK), BLK), :]
        )
        return carry

    lax.fori_loop(0, NB * NNZB, one_block, 0, unroll=4)


def first_kernel(here, k_cols, h_cols, *refs, resident):
    phi, dense_k, product, dense_h, k_blocks, h_blocks, sems = refs[-7:]
    parts = refs[:-7]
    last = 2 * SIDES[0]

    def copies(which):
        target = (k_blocks, h_blocks)[which]
        if not resident:
            return [pltpu.make_async_copy(parts[which], target, sems.at[which, 0, 0])]
        out_list = []
        if which == 0:
            columns = SIDES[1] * SIDES[2]
            for n, (part, core, piece, column) in enumerate(block_places(here, parts[:-last])):
                depth = part.shape[-2]
                for z in range(SIDES[0]):
                    row = (((core * SIDES[0] + z) * columns + column) * PIECES + piece) * depth
                    out_list.append(
                        pltpu.make_async_copy(
                            part.at[z],
                            target.at[pl.ds(pl.multiple_of(row, depth), depth)],
                            sems.at[which, n, z],
                        )
                    )
            return out_list
        depth = parts[-1].shape[-2]
        rep, y, x, z = (here[k] for k in range(4))
        for n, part in enumerate(parts[-last:]):
            core = rep if n < SIDES[0] else 1 - rep
            level = lax.rem(z + SIDES[0] - n % SIDES[0], SIDES[0])
            for c in range(SIDES[1] * SIDES[2]):
                to_y = y if c < 2 else 1 - y
                to_x = x if c % 2 == 0 else 1 - x
                row = (((core * SIDES[0] + level) * SIDES[1] + to_y) * SIDES[2] + to_x) * depth
                out_list.append(
                    pltpu.make_async_copy(
                        part.at[c],
                        target.at[pl.ds(pl.multiple_of(row, depth), depth)],
                        sems.at[which, n, c],
                    )
                )
        return out_list

    @pl.when(pl.program_id(0) == 0)
    def _():
        for which in range(2):
            for copy in copies(which):
                copy.start()
        for which, (cols, blocks, dense) in enumerate(
            ((k_cols, k_blocks, dense_k), (h_cols, h_blocks, dense_h))
        ):
            for copy in copies(which):
                copy.wait()
            dense_rows(cols, blocks, dense)

    kphi = jnp.dot(dense_k[...], phi[...], preferred_element_type=jnp.float32)
    product[...] = jnp.dot(
        dense_h[...], kphi.astype(jnp.bfloat16), preferred_element_type=jnp.float32
    )


def first_products(here, k_cols, h_cols, parts, phi, resident):
    width = phi.shape[1]
    tile = min(COLS, width)
    stored = pltpu.VMEM((NB * NNZB * BLK, BLK), jnp.bfloat16)
    grid_spec = pltpu.PrefetchScalarGridSpec(
        num_scalar_prefetch=3,
        grid=(width // tile,),
        in_specs=[pl.BlockSpec(memory_space=pl.ANY)] * len(parts)
        + [pl.BlockSpec((NF, tile), lambda i, *s: (0, i))],
        out_specs=[
            pl.BlockSpec((NF, NF), lambda i, *s: (0, 0)),
            pl.BlockSpec((NF, tile), lambda i, *s: (0, i)),
        ],
        scratch_shapes=[
            pltpu.VMEM((NF, NF), jnp.bfloat16),
            stored,
            stored,
            pltpu.SemaphoreType.DMA((2, len(parts), SIDES[1] * SIDES[2])),
        ],
    )
    return pl.pallas_call(
        functools.partial(first_kernel, resident=resident),
        out_shape=[
            jax.ShapeDtypeStruct((NF, NF), jnp.bfloat16),
            jax.ShapeDtypeStruct((NF, width), jnp.float32),
        ],
        grid_spec=grid_spec,
        compiler_params=pltpu.CompilerParams(vmem_limit_bytes=VMEM),
        name="products",
        cost_estimate=pl.CostEstimate(
            flops=4 * NF * NF * width, bytes_accessed=24 << 20, transcendentals=0
        ),
    )(here, k_cols, h_cols, *parts, phi)


def last_kernel(dense_k, hphi, product, out):
    ydiff = (hphi[...].astype(jnp.float32) - product[...]).astype(jnp.bfloat16)
    out[...] = jnp.dot(dense_k[...], ydiff, preferred_element_type=jnp.float32).astype(jnp.bfloat16)


def last_product(dense_k, hphi, product):
    width = hphi.shape[1]
    tile = min(COLS, width)
    columns = pl.BlockSpec((NF, tile), lambda i: (0, i))
    return pl.pallas_call(
        last_kernel,
        out_shape=jax.ShapeDtypeStruct((NF, width), jnp.bfloat16),
        grid=(width // tile,),
        in_specs=[pl.BlockSpec((NF, NF), lambda i: (0, 0)), columns, columns],
        out_specs=columns,
        compiler_params=pltpu.CompilerParams(vmem_limit_bytes=VMEM),
        name="gradient",
        cost_estimate=pl.CostEstimate(
            flops=2 * NF * NF * width, bytes_accessed=17 << 20, transcendentals=0
        ),
    )(dense_k, hphi, product)


def place_of():
    me = lax.axis_index("func")
    return me // 4, (me // 2) % 2, me % 2


def along_z(part):
    z = place_of()[0]
    n = lax.axis_size("func")
    held = [part]
    for k in range(1, 4):
        held.append(lax.ppermute(part, "func", [(i, (i + 4 * k) % n) for i in range(n)]))

    def at(level):
        taken = held[0]
        for k in range(1, 4):
            taken = jnp.where((z - level) % 4 == k, held[k], taken)
        return taken

    return jnp.stack([at(level) for level in range(4)])


def swapped(block, bit):
    n = lax.axis_size("func")
    return lax.ppermute(block, "func", [(i, i ^ bit) for i in range(n)])


def onward(block, step, up):
    n = lax.axis_size("func")
    plane = n // SIDES[0]
    if up:
        route = [(i, i + plane) for i in range(plane * (step - 1), n - plane)]
    else:
        route = [(i, i - plane) for i in range(plane, n - plane * (step - 1))]
    return lax.ppermute(block, "func", route)


def ordered(lines, near, far):
    blocks = []
    for p, (line, close, (apart, corner)) in enumerate(zip(lines, near, far)):
        middle = [close, apart] if p % 2 == 0 else [apart, close]
        blocks += [line, *middle, corner]
    return blocks


def other_core(block):
    return lax.ppermute(block, "rep", [(0, 1), (1, 0)])


def shards(orbitals, centres, potential, kernel, kernel_cols, hamiltonian, intersection_cols):
    rep = lax.axis_index("rep")
    n_func = lax.axis_size("func")
    n_rep = lax.axis_size("rep")
    owned, planes, flat = orbitals.shape
    z_planes, x_size, y_size = potential.shape
    shares = n_func // planes
    width = flat // shares
    x_blocks = x_size // n_rep // ROWS

    def exchange(rows):
        return lax.all_to_all(rows, "func", split_axis=0, concat_axis=0, tiled=True)

    def cut(plane_rows):
        pieces = plane_rows.reshape(planes, owned, shares, width).transpose(0, 2, 1, 3)
        return pieces.reshape(n_func, owned, width)

    half = lax.dynamic_slice_in_dim(potential, rep * (x_size // n_rep), x_size // n_rep, axis=1)
    half = half.astype(jnp.bfloat16).reshape(z_planes, x_blocks, ROWS, y_size).transpose(1, 0, 2, 3)
    phi_planes = orbitals.transpose(1, 0, 2)
    phi_cut = cut(phi_planes)
    edge = jnp.where(rep == 0, phi_planes[planes - 2 :], phi_planes[:2])
    halo = lax.ppermute(edge, "rep", [(0, 1), (1, 0)])
    info = jnp.concatenate([centres[:, :1] + planes * rep, centres[:, 1:]], axis=1)
    info = info.astype(jnp.int32)
    band = planar_band()

    resident = n_func == SIDES[0] * SIDES[1] * SIDES[2]
    if resident:
        level, y, x = place_of()
        here = jnp.stack([rep, y, x, level]).astype(jnp.int32)
        per = x_blocks // PIECES
        lines = [along_z(half[p * per : (p + 1) * per]) for p in range(PIECES)]
        h_own = hamiltonian[0]
        h_near, h_apart = swapped(h_own, 1), swapped(h_own, 2)
        around = jnp.stack([h_own, h_near, h_apart, swapped(h_near, 2)])
        lines, around, kernel, halo, band, info, phi_cut = lax.optimization_barrier(
            (lines, around, kernel, halo, band, info, phi_cut)
        )
        near = [swapped(lines[p], 1 + p) for p in range(PIECES)]
        ups, downs = [onward(around, 1, True)], [onward(around, 1, False)]
        k_line = along_z(kernel[0])
        lines_too = [other_core(block) for block in lines]
        near, ups, downs, k_line = lax.optimization_barrier((near, ups, downs, k_line))
        far = [(swapped(lines[p], 2 - p), swapped(near[p], 2 - p)) for p in range(PIECES)]
        ups.append(onward(ups[0], 2, True))
        downs.append(onward(downs[0], 2, False))
        rows_of = k_line.shape[1] // PIECES
        k_lines = [k_line[:, p * rows_of : (p + 1) * rows_of] for p in range(PIECES)]
        k_near = [swapped(k_lines[p], 1 + p) for p in range(PIECES)]
        near_too = [other_core(block) for block in near]
        ups.append(onward(ups[1], 3, True))
        downs.append(onward(downs[1], 3, False))
        far_too = [tuple(other_core(block) for block in pair) for pair in far]
        far, ups, downs, k_near, phi_cut, lines_too, near_too = lax.optimization_barrier(
            (far, ups, downs, k_near, phi_cut, lines_too, near_too)
        )
        phi_pts = exchange(phi_cut)
        k_far = [(swapped(k_lines[p], 2 - p), swapped(k_near[p], 2 - p)) for p in range(PIECES)]
        pot = ordered(lines, near, far) + ordered(lines_too, near_too, far_too)
        h_parts = [around]
        for k in range(1, SIDES[0]):
            h_parts.append(jnp.where(level >= k, ups[k - 1], downs[SIDES[0] - 1 - k]))
        h_parts = h_parts + [other_core(part) for part in h_parts]
    else:
        here = jnp.stack([rep, rep, rep, rep]).astype(jnp.int32)
        pot = lax.all_gather(half, ("rep", "func"), axis=0, tiled=False)
        pot = pot.reshape(n_rep, n_func, x_blocks, z_planes, ROWS, y_size)
        pot = pot.transpose(0, 2, 1, 3, 4, 5)
        pot = [pot.reshape(n_rep, x_blocks, n_func * z_planes, ROWS, y_size)]
        phi_pts = exchange(phi_cut)
        parts = [
            lax.all_gather(stored, ("rep", "func"), axis=1, tiled=True).reshape(-1, BLK)
            for stored in (kernel, hamiltonian)
        ]

    extra = -owned % GROUP
    padded = [
        jnp.pad(info, ((0, extra), (0, 0))),
        jnp.pad(phi_planes, ((0, 0), (0, extra), (0, 0))),
        jnp.pad(halo, ((0, 0), (0, extra), (0, 0))),
    ]
    info, phi_planes, halo = padded
    hphi = make_hphi(info, here, phi_planes, halo, band, pot, resident)[:, :owned]
    if resident:
        hphi, k_far = lax.optimization_barrier((hphi, k_far))
        k_parts = ordered(k_lines, k_near, k_far)
        parts = k_parts + [other_core(part) for part in k_parts] + h_parts
    phi_pts = phi_pts.reshape(n_func * owned, width)
    dense_k, product = first_products(
        here, kernel_cols, intersection_cols, parts, phi_pts, resident
    )
    hphi_pts = exchange(cut(hphi)).reshape(n_func * owned, width)
    gradient = last_product(dense_k, hphi_pts, product)
    back = exchange(gradient.reshape(n_func, owned, width))
    back = back.reshape(planes, shares, owned, width).transpose(2, 0, 1, 3)
    return back.reshape(owned, planes, flat)


def solution(mesh):
    placed = (
        P("func", "rep", None),
        P("func", None),
        P("func", None, None),
        P("rep", "func", None),
        P(),
        P("rep", "func", None),
        P(),
    )
    return jax.shard_map(
        shards, mesh=mesh, in_specs=placed, out_specs=P("func", "rep", None), check_vma=False
    )
```

```python
import functools

import jax
import jax.numpy as jnp
from jax import lax
from jax.experimental import pallas as pl
from jax.experimental.pallas import tpu as pltpu
from jax.sharding import PartitionSpec as P

BOX = 32
BLK = 128
NNZB = 12
NB = 12
NF = NB * BLK
LANES = 128
ROWS = 16
GROUP = 16
COLS = 256
VMEM = 56 * 1024 * 1024
SLOTS = 8
PIECES = 2

CENTRE = 90.0
NEAR = -16.0
FAR = 1.0
SCALE = 1.0 / 96.0


SIDES = (4, 2, 2)


def block_places(here, blocks, pieces=PIECES):
    rep, y, x = (here[k] for k in range(3))
    places = []
    for n, block in enumerate(blocks):
        core = rep if n < len(blocks) // 2 else 1 - rep
        piece = n // 4 % pieces
        to_y = y if n % 4 < 2 else 1 - y
        to_x = x if n % 2 == 0 else 1 - x
        places.append((block, core, piece, to_y * SIDES[2] + to_x))
    return places


def planar_band():
    row = lax.broadcasted_iota(jnp.int32, (2 * COLS, COLS), 0) - LANES
    col = lax.broadcasted_iota(jnp.int32, (2 * COLS, COLS), 1)
    across = jnp.abs((row + LANES) // BOX - (col + LANES) // BOX)
    along = jnp.abs((row + LANES) % BOX - (col + LANES) % BOX)
    band = jnp.zeros((2 * COLS, COLS), jnp.float32)
    for one, other in ((across, along), (along, across)):
        band = jnp.where((one == 0) & (other == 1), NEAR, band)
        band = jnp.where((one == 0) & (other == 2), FAR, band)
    band = jnp.where((across == 0) & (along == 0), CENTRE, band)
    return band.astype(jnp.bfloat16)


def hphi_kernel(info, here, phi, halo, band, *refs, resident):
    planes, group, flat = phi.shape
    step = pl.program_id(0)
    total = pl.num_programs(0) * group
    span = 3 * ROWS
    flag = here[0].astype(jnp.float32)
    if resident:
        blocks, (out, pot, rows, win, sems) = refs[:-5], refs[-5:]
    else:
        pot, out, buf, rows, win, sems = refs
    x_blocks = pot.shape[1]

    def copies(index, slot):
        z = info[index, 0]
        first = info[index, 1] // ROWS
        out_list = []
        for k in range(3):
            block = lax.rem(first + k, 2 * x_blocks)
            out_list.append(
                pltpu.make_async_copy(
                    pot.at[block // x_blocks, lax.rem(block, x_blocks), pl.ds(z, planes)],
                    buf.at[slot, k],
                    sems.at[slot, k],
                )
            )
        return out_list

    @pl.when(step == 0)
    def _():
        if resident:
            started = []
            for n, (block, core, piece, column) in enumerate(block_places(here, blocks)):
                per, depth = block.shape[1:3]
                for z in range(SIDES[0]):
                    target = pl.multiple_of((z * SIDES[1] * SIDES[2] + column) * depth, depth)
                    started.append(
                        pltpu.make_async_copy(
                            block.at[z],
                            pot.at[core, pl.ds(piece * per, per), pl.ds(target, depth)],
                            sems.at[n, z],
                        )
                    )
            for copy in started:
                copy.start()
            for copy in started:
                copy.wait()
        else:
            for early in range(SLOTS - 1):
                for copy in copies(early, early):
                    copy.start()

    lane = lax.broadcasted_iota(jnp.int32, (8, LANES), 1)

    def one_function(f, carry):
        index = step * group + f
        if resident:
            z0 = info[index, 0]
            first = info[index, 1] // ROWS
            for k in range(3):
                block = lax.rem(first + k, 2 * x_blocks)
                source = pot.at[block // x_blocks, lax.rem(block, x_blocks)]
                for z in range(planes):
                    rows[pl.ds(z * span + k * ROWS, ROWS), :] = source[z0 + z].astype(jnp.float32)
        else:
            slot = lax.rem(index, SLOTS)
            ahead = index + SLOTS - 1

            @pl.when(ahead < total)
            def _():
                for copy in copies(ahead, lax.rem(ahead, SLOTS)):
                    copy.start()

            for copy in copies(index, slot):
                copy.wait()
            for z in range(planes):
                for k in range(3):
                    rows[pl.ds(z * span + k * ROWS, ROWS), :] = buf[slot, k, z].astype(jnp.float32)
        shift_x = lax.rem(info[index, 1], ROWS)
        shift_y = info[index, 2]
        for z in range(planes):
            value = None
            for b in range(4):
                part = rows[pl.ds(z * span + b + shift_x, 8, stride=4), :]
                part = pltpu.roll(part, lax.rem(b * BOX + LANES - shift_y, LANES), axis=1)
                value = part if value is None else jnp.where(lane >= b * BOX, part, value)
            win[pl.ds(z * group + f, 8, stride=planes * group), :] = value
        return carry

    lax.fori_loop(0, group, one_function, 0)

    pieces = flat // COLS
    for c in range(pieces):
        low = max(0, c * COLS - LANES)
        high = min(flat, c * COLS + COLS + LANES)
        cols = slice(c * COLS, (c + 1) * COLS)
        left = phi[:, :, low:high].reshape(planes * group, high - low)
        base = low - (c * COLS - LANES)
        planar = jnp.dot(
            left, band[base : base + high - low, :], preferred_element_type=jnp.float32
        )
        level = [phi[z, :, cols].astype(jnp.float32) for z in range(planes)]
        other = [halo[h, :, cols].astype(jnp.float32) for h in range(2)]
        below = [h * flag for h in other]
        above = [h * (1.0 - flag) for h in other]
        level = below + level + above
        for z in range(planes):
            kin = planar[z * group : (z + 1) * group]
            kin = kin + NEAR * (level[z + 1] + level[z + 3]) + FAR * (level[z] + level[z + 4])
            w = jnp.concatenate(
                [
                    win[pl.ds((a * planes + z) * group, group), :]
                    for a in range(c * COLS // LANES, (c + 1) * COLS // LANES)
                ],
                axis=1,
            )
            vphi = (w * level[z + 2]).astype(jnp.bfloat16).astype(jnp.float32)
            out[z, :, cols] = (SCALE * kin + vphi).astype(jnp.bfloat16)


def make_hphi(info, here, phi, halo, band, blocks, resident):
    planes, owned, flat = phi.shape
    span = 3 * ROWS
    if resident:
        per, depth = blocks[0].shape[1:3]
        size = (2, PIECES * per, SIDES[0] * SIDES[1] * SIDES[2] * depth, ROWS, LANES)
        taken = pltpu.VMEM(size, jnp.bfloat16)
        sems = pltpu.SemaphoreType.DMA((len(blocks), SIDES[0]))
    else:
        taken = pltpu.VMEM((SLOTS, 3, planes, ROWS, LANES), jnp.bfloat16)
        sems = pltpu.SemaphoreType.DMA((SLOTS, 3))
    grid_spec = pltpu.PrefetchScalarGridSpec(
        num_scalar_prefetch=2,
        grid=(owned // GROUP,),
        in_specs=[
            pl.BlockSpec((planes, GROUP, flat), lambda i, s, t: (0, i, 0)),
            pl.BlockSpec((2, GROUP, flat), lambda i, s, t: (0, i, 0)),
            pl.BlockSpec(band.shape, lambda i, s, t: (0, 0)),
        ]
        + [pl.BlockSpec(memory_space=pl.ANY)] * len(blocks),
        out_specs=pl.BlockSpec((planes, GROUP, flat), lambda i, s, t: (0, i, 0)),
        scratch_shapes=[
            taken,
            pltpu.VMEM((planes * span, LANES), jnp.float32),
            pltpu.VMEM((flat // LANES * planes * GROUP, LANES), jnp.float32),
            sems,
        ],
    )
    return pl.pallas_call(
        functools.partial(hphi_kernel, resident=resident),
        out_shape=jax.ShapeDtypeStruct((planes, owned, flat), jnp.bfloat16),
        grid_spec=grid_spec,
        compiler_params=pltpu.CompilerParams(vmem_limit_bytes=VMEM),
        name="hphi",
        cost_estimate=pl.CostEstimate(
            flops=8 * planes * owned * flat * flat, bytes_accessed=60 << 20, transcendentals=0
        ),
    )(info, here, phi, halo, band, *blocks)


def dense_rows(cols, blocks, dense):
    def one_block(n, carry):
        i = n // NNZB
        col = cols[i, lax.rem(n, NNZB)]
        dense[pl.ds(pl.multiple_of(i * BLK, BLK), BLK), pl.ds(pl.multiple_of(col * BLK, BLK), BLK)] = (
            blocks[pl.ds(pl.multiple_of(n * BLK, BLK), BLK), :]
        )
        return carry

    lax.fori_loop(0, NB * NNZB, one_block, 0, unroll=4)


def first_kernel(here, k_cols, h_cols, *refs):
    phi, dense_k, product, dense_h, k_blocks, h_blocks, sems = refs[-7:]
    half = (len(refs) - 7) // 2
    depth = refs[0].shape[-2]

    def copies(which):
        stored = refs[which * half : (which + 1) * half]
        target = (k_blocks, h_blocks)[which]
        if half == 1:
            return [pltpu.make_async_copy(stored[0], target, sems.at[which, 0, 0])]
        out_list = []
        columns = SIDES[1] * SIDES[2]
        for n, (block, core, _, column) in enumerate(block_places(here, stored, 1)):
            for z in range(SIDES[0]):
                row = ((core * SIDES[0] + z) * columns + column) * depth
                out_list.append(
                    pltpu.make_async_copy(
                        block.at[z],
                        target.at[pl.ds(pl.multiple_of(row, depth), depth)],
                        sems.at[which, n, z],
                    )
                )
        return out_list

    @pl.when(pl.program_id(0) == 0)
    def _():
        for which in range(2):
            for copy in copies(which):
                copy.start()
        for which, (cols, blocks, dense) in enumerate(
            ((k_cols, k_blocks, dense_k), (h_cols, h_blocks, dense_h))
        ):
            for copy in copies(which):
                copy.wait()
            dense_rows(cols, blocks, dense)

    kphi = jnp.dot(dense_k[...], phi[...], preferred_element_type=jnp.float32)
    product[...] = jnp.dot(
        dense_h[...], kphi.astype(jnp.bfloat16), preferred_element_type=jnp.float32
    )


def first_products(here, k_cols, h_cols, k_parts, h_parts, phi):
    width = phi.shape[1]
    tile = min(COLS, width)
    stored = pltpu.VMEM((NB * NNZB * BLK, BLK), jnp.bfloat16)
    grid_spec = pltpu.PrefetchScalarGridSpec(
        num_scalar_prefetch=3,
        grid=(width // tile,),
        in_specs=[pl.BlockSpec(memory_space=pl.ANY)] * (2 * len(k_parts))
        + [pl.BlockSpec((NF, tile), lambda i, *s: (0, i))],
        out_specs=[
            pl.BlockSpec((NF, NF), lambda i, *s: (0, 0)),
            pl.BlockSpec((NF, tile), lambda i, *s: (0, i)),
        ],
        scratch_shapes=[
            pltpu.VMEM((NF, NF), jnp.bfloat16),
            stored,
            stored,
            pltpu.SemaphoreType.DMA((2, len(k_parts), SIDES[0])),
        ],
    )
    return pl.pallas_call(
        first_kernel,
        out_shape=[
            jax.ShapeDtypeStruct((NF, NF), jnp.bfloat16),
            jax.ShapeDtypeStruct((NF, width), jnp.float32),
        ],
        grid_spec=grid_spec,
        compiler_params=pltpu.CompilerParams(vmem_limit_bytes=VMEM),
        name="products",
        cost_estimate=pl.CostEstimate(
            flops=4 * NF * NF * width, bytes_accessed=24 << 20, transcendentals=0
        ),
    )(here, k_cols, h_cols, *k_parts, *h_parts, phi)


def last_kernel(dense_k, hphi, product, out):
    ydiff = (hphi[...].astype(jnp.float32) - product[...]).astype(jnp.bfloat16)
    out[...] = jnp.dot(dense_k[...], ydiff, preferred_element_type=jnp.float32).astype(jnp.bfloat16)


def last_product(dense_k, hphi, product):
    width = hphi.shape[1]
    tile = min(COLS, width)
    columns = pl.BlockSpec((NF, tile), lambda i: (0, i))
    return pl.pallas_call(
        last_kernel,
        out_shape=jax.ShapeDtypeStruct((NF, width), jnp.bfloat16),
        grid=(width // tile,),
        in_specs=[pl.BlockSpec((NF, NF), lambda i: (0, 0)), columns, columns],
        out_specs=columns,
        compiler_params=pltpu.CompilerParams(vmem_limit_bytes=VMEM),
        name="gradient",
        cost_estimate=pl.CostEstimate(
            flops=2 * NF * NF * width, bytes_accessed=17 << 20, transcendentals=0
        ),
    )(dense_k, hphi, product)


def place_of():
    me = lax.axis_index("func")
    return me // 4, (me // 2) % 2, me % 2


def along_z(part, cuts):
    z = place_of()[0]
    n = lax.axis_size("func")
    held = [part]
    for k in range(1, 4):
        held.append(lax.ppermute(part, "func", [(i, (i + 4 * k) % n) for i in range(n)]))
    size = part.shape[0] // cuts

    def at(level, first):
        taken = held[0][first : first + size]
        for k in range(1, 4):
            taken = jnp.where((z - level) % 4 == k, held[k][first : first + size], taken)
        return taken

    return [jnp.stack([at(level, c * size) for level in range(4)]) for c in range(cuts)]


def swapped(block, bit):
    n = lax.axis_size("func")
    return lax.ppermute(block, "func", [(i, i ^ bit) for i in range(n)])


def ordered(lines, near, far, first=0):
    blocks = []
    for p, (line, close, (apart, corner)) in enumerate(zip(lines, near, far)):
        middle = [close, apart] if (p + first) % 2 == 0 else [apart, close]
        blocks += [line, *middle, corner]
    return blocks


def other_core(block):
    return lax.ppermute(block, "rep", [(0, 1), (1, 0)])


def shards(orbitals, centres, potential, kernel, kernel_cols, hamiltonian, intersection_cols):
    rep = lax.axis_index("rep")
    n_func = lax.axis_size("func")
    n_rep = lax.axis_size("rep")
    owned, planes, flat = orbitals.shape
    z_planes, x_size, y_size = potential.shape
    shares = n_func // planes
    width = flat // shares
    x_blocks = x_size // n_rep // ROWS

    def exchange(rows):
        return lax.all_to_all(rows, "func", split_axis=0, concat_axis=0, tiled=True)

    def cut(plane_rows):
        pieces = plane_rows.reshape(planes, owned, shares, width).transpose(0, 2, 1, 3)
        return pieces.reshape(n_func, owned, width)

    half = lax.dynamic_slice_in_dim(potential, rep * (x_size // n_rep), x_size // n_rep, axis=1)
    half = half.astype(jnp.bfloat16).reshape(z_planes, x_blocks, ROWS, y_size).transpose(1, 0, 2, 3)
    phi_planes = orbitals.transpose(1, 0, 2)
    phi_cut = cut(phi_planes)
    edge = jnp.where(rep == 0, phi_planes[planes - 2 :], phi_planes[:2])
    halo = lax.ppermute(edge, "rep", [(0, 1), (1, 0)])
    info = jnp.concatenate([centres[:, :1] + planes * rep, centres[:, 1:]], axis=1)
    info = info.astype(jnp.int32)
    band = planar_band()

    resident = n_func == SIDES[0] * SIDES[1] * SIDES[2]
    if resident:
        _, y, x = place_of()
        here = jnp.stack([rep, y, x]).astype(jnp.int32)
        lines = along_z(half, PIECES)
        stored = jnp.concatenate([kernel[0], hamiltonian[0]])
        lines, stored, halo, band, info, phi_cut = lax.optimization_barrier(
            (lines, stored, halo, band, info, phi_cut)
        )
        near = [swapped(lines[p], 1 + p) for p in range(PIECES)]
        matrix_lines = along_z(stored, 2)
        lines_too = [other_core(block) for block in lines]
        near, matrix_lines, lines_too = lax.optimization_barrier((near, matrix_lines, lines_too))
        far = [(swapped(lines[p], 2 - p), swapped(near[p], 2 - p)) for p in range(PIECES)]
        near_too = [other_core(block) for block in near]
        far_too = [tuple(other_core(block) for block in pair) for pair in far]
        far, matrix_lines, phi_cut, near_too = lax.optimization_barrier(
            (far, matrix_lines, phi_cut, near_too)
        )
        phi_pts = exchange(phi_cut)
        matrix_near = [swapped(matrix_lines[p], 1 + p) for p in range(2)]
        matrix_near, info = lax.optimization_barrier((matrix_near, info))
        matrix_far = [
            (swapped(matrix_lines[p], 2 - p), swapped(matrix_near[p], 2 - p)) for p in range(2)
        ]
        pot = ordered(lines, near, far) + ordered(lines_too, near_too, far_too)
    else:
        here = jnp.stack([rep, rep, rep]).astype(jnp.int32)
        pot = lax.all_gather(half, ("rep", "func"), axis=0, tiled=False)
        pot = pot.reshape(n_rep, n_func, x_blocks, z_planes, ROWS, y_size)
        pot = pot.transpose(0, 2, 1, 3, 4, 5)
        pot = [pot.reshape(n_rep, x_blocks, n_func * z_planes, ROWS, y_size)]
        phi_pts = exchange(phi_cut)
        k_parts, h_parts = (
            [lax.all_gather(stored, ("rep", "func"), axis=1, tiled=True).reshape(-1, BLK)]
            for stored in (kernel, hamiltonian)
        )

    extra = -owned % GROUP
    padded = [
        jnp.pad(info, ((0, extra), (0, 0))),
        jnp.pad(phi_planes, ((0, 0), (0, extra), (0, 0))),
        jnp.pad(halo, ((0, 0), (0, extra), (0, 0))),
    ]
    info, phi_planes, halo = padded
    hphi = make_hphi(info, here, phi_planes, halo, band, pot, resident)[:, :owned]
    if resident:
        hphi, matrix_far = lax.optimization_barrier((hphi, matrix_far))
        k_parts, h_parts = (
            ordered(matrix_lines[p : p + 1], matrix_near[p : p + 1], matrix_far[p : p + 1], p)
            for p in range(2)
        )
        k_parts = k_parts + [other_core(block) for block in k_parts]
        h_parts = h_parts + [other_core(block) for block in h_parts]
    phi_pts = phi_pts.reshape(n_func * owned, width)
    dense_k, product = first_products(
        here, kernel_cols, intersection_cols, k_parts, h_parts, phi_pts
    )
    hphi_pts = exchange(cut(hphi)).reshape(n_func * owned, width)
    gradient = last_product(dense_k, hphi_pts, product)
    back = exchange(gradient.reshape(n_func, owned, width))
    back = back.reshape(planes, shares, owned, width).transpose(2, 0, 1, 3)
    return back.reshape(owned, planes, flat)


def solution(mesh):
    placed = (
        P("func", "rep", None),
        P("func", None),
        P("func", None, None),
        P("rep", "func", None),
        P(),
        P("rep", "func", None),
        P(),
    )
    return jax.shard_map(
        shards, mesh=mesh, in_specs=placed, out_specs=P("func", "rep", None), check_vma=False
    )
```

```python
import functools

import jax
import jax.numpy as jnp
from jax import lax
from jax.experimental import pallas as pl
from jax.experimental.pallas import tpu as pltpu
from jax.sharding import PartitionSpec as P

BOX = 32
BLK = 128
NNZB = 12
NB = 12
NF = NB * BLK
LANES = 128
ROWS = 16
GROUP = 16
COLS = 256
VMEM = 56 * 1024 * 1024
SLOTS = 8
PIECES = 2

CENTRE = 90.0
NEAR = -16.0
FAR = 1.0
SCALE = 1.0 / 96.0


SIDES = (4, 2, 2)


def block_places(here, blocks, pieces=PIECES):
    rep, y, x = (here[k] for k in range(3))
    places = []
    for n, block in enumerate(blocks):
        core = rep if n < len(blocks) // 2 else 1 - rep
        piece = n // 4 % pieces
        to_y = y if n % 4 < 2 else 1 - y
        to_x = x if n % 2 == 0 else 1 - x
        places.append((block, core, piece, to_y * SIDES[2] + to_x))
    return places


def planar_band():
    row = lax.broadcasted_iota(jnp.int32, (2 * COLS, COLS), 0) - LANES
    col = lax.broadcasted_iota(jnp.int32, (2 * COLS, COLS), 1)
    across = jnp.abs((row + LANES) // BOX - (col + LANES) // BOX)
    along = jnp.abs((row + LANES) % BOX - (col + LANES) % BOX)
    band = jnp.zeros((2 * COLS, COLS), jnp.float32)
    for one, other in ((across, along), (along, across)):
        band = jnp.where((one == 0) & (other == 1), NEAR, band)
        band = jnp.where((one == 0) & (other == 2), FAR, band)
    band = jnp.where((across == 0) & (along == 0), CENTRE, band)
    return band.astype(jnp.bfloat16)


def hphi_kernel(info, here, phi, halo, band, *refs, resident):
    planes, group, flat = phi.shape
    step = pl.program_id(0)
    total = pl.num_programs(0) * group
    span = 3 * ROWS
    flag = here[0].astype(jnp.float32)
    if resident:
        blocks, (out, pot, rows, win, sems) = refs[:-5], refs[-5:]
    else:
        pot, out, buf, rows, win, sems = refs
    x_blocks = pot.shape[1]

    def copies(index, slot):
        z = info[index, 0]
        first = info[index, 1] // ROWS
        out_list = []
        for k in range(3):
            block = lax.rem(first + k, 2 * x_blocks)
            out_list.append(
                pltpu.make_async_copy(
                    pot.at[block // x_blocks, lax.rem(block, x_blocks), pl.ds(z, planes)],
                    buf.at[slot, k],
                    sems.at[slot, k],
                )
            )
        return out_list

    @pl.when(step == 0)
    def _():
        if resident:
            started = []
            for n, (block, core, piece, column) in enumerate(block_places(here, blocks)):
                per, depth = block.shape[1:3]
                for z in range(SIDES[0]):
                    target = pl.multiple_of((z * SIDES[1] * SIDES[2] + column) * depth, depth)
                    started.append(
                        pltpu.make_async_copy(
                            block.at[z],
                            pot.at[core, pl.ds(piece * per, per), pl.ds(target, depth)],
                            sems.at[n, z],
                        )
                    )
            for copy in started:
                copy.start()
            for copy in started:
                copy.wait()
        else:
            for early in range(SLOTS - 1):
                for copy in copies(early, early):
                    copy.start()

    lane = lax.broadcasted_iota(jnp.int32, (8, LANES), 1)

    def one_function(f, carry):
        index = step * group + f
        if resident:
            z0 = info[index, 0]
            first = info[index, 1] // ROWS
            for k in range(3):
                block = lax.rem(first + k, 2 * x_blocks)
                source = pot.at[block // x_blocks, lax.rem(block, x_blocks)]
                for z in range(planes):
                    rows[pl.ds(z * span + k * ROWS, ROWS), :] = source[z0 + z].astype(jnp.float32)
        else:
            slot = lax.rem(index, SLOTS)
            ahead = index + SLOTS - 1

            @pl.when(ahead < total)
            def _():
                for copy in copies(ahead, lax.rem(ahead, SLOTS)):
                    copy.start()

            for copy in copies(index, slot):
                copy.wait()
            for z in range(planes):
                for k in range(3):
                    rows[pl.ds(z * span + k * ROWS, ROWS), :] = buf[slot, k, z].astype(jnp.float32)
        shift_x = lax.rem(info[index, 1], ROWS)
        shift_y = info[index, 2]
        for z in range(planes):
            value = None
            for b in range(4):
                part = rows[pl.ds(z * span + b + shift_x, 8, stride=4), :]
                part = pltpu.roll(part, lax.rem(b * BOX + LANES - shift_y, LANES), axis=1)
                value = part if value is None else jnp.where(lane >= b * BOX, part, value)
            win[pl.ds(z * group + f, 8, stride=planes * group), :] = value
        return carry

    lax.fori_loop(0, group, one_function, 0)

    pieces = flat // COLS
    for c in range(pieces):
        low = max(0, c * COLS - LANES)
        high = min(flat, c * COLS + COLS + LANES)
        cols = slice(c * COLS, (c + 1) * COLS)
        left = phi[:, :, low:high].reshape(planes * group, high - low)
        base = low - (c * COLS - LANES)
        planar = jnp.dot(
            left, band[base : base + high - low, :], preferred_element_type=jnp.float32
        )
        level = [phi[z, :, cols].astype(jnp.float32) for z in range(planes)]
        other = [halo[h, :, cols].astype(jnp.float32) for h in range(2)]
        below = [h * flag for h in other]
        above = [h * (1.0 - flag) for h in other]
        level = below + level + above
        for z in range(planes):
            kin = planar[z * group : (z + 1) * group]
            kin = kin + NEAR * (level[z + 1] + level[z + 3]) + FAR * (level[z] + level[z + 4])
            w = jnp.concatenate(
                [
                    win[pl.ds((a * planes + z) * group, group), :]
                    for a in range(c * COLS // LANES, (c + 1) * COLS // LANES)
                ],
                axis=1,
            )
            vphi = (w * level[z + 2]).astype(jnp.bfloat16).astype(jnp.float32)
            out[z, :, cols] = (SCALE * kin + vphi).astype(jnp.bfloat16)


def make_hphi(info, here, phi, halo, band, blocks, resident):
    planes, owned, flat = phi.shape
    span = 3 * ROWS
    if resident:
        per, depth = blocks[0].shape[1:3]
        size = (2, PIECES * per, SIDES[0] * SIDES[1] * SIDES[2] * depth, ROWS, LANES)
        taken = pltpu.VMEM(size, jnp.bfloat16)
        sems = pltpu.SemaphoreType.DMA((len(blocks), SIDES[0]))
    else:
        taken = pltpu.VMEM((SLOTS, 3, planes, ROWS, LANES), jnp.bfloat16)
        sems = pltpu.SemaphoreType.DMA((SLOTS, 3))
    grid_spec = pltpu.PrefetchScalarGridSpec(
        num_scalar_prefetch=2,
        grid=(owned // GROUP,),
        in_specs=[
            pl.BlockSpec((planes, GROUP, flat), lambda i, s, t: (0, i, 0)),
            pl.BlockSpec((2, GROUP, flat), lambda i, s, t: (0, i, 0)),
            pl.BlockSpec(band.shape, lambda i, s, t: (0, 0)),
        ]
        + [pl.BlockSpec(memory_space=pl.ANY)] * len(blocks),
        out_specs=pl.BlockSpec((planes, GROUP, flat), lambda i, s, t: (0, i, 0)),
        scratch_shapes=[
            taken,
            pltpu.VMEM((planes * span, LANES), jnp.float32),
            pltpu.VMEM((flat // LANES * planes * GROUP, LANES), jnp.float32),
            sems,
        ],
    )
    return pl.pallas_call(
        functools.partial(hphi_kernel, resident=resident),
        out_shape=jax.ShapeDtypeStruct((planes, owned, flat), jnp.bfloat16),
        grid_spec=grid_spec,
        compiler_params=pltpu.CompilerParams(vmem_limit_bytes=VMEM),
        name="hphi",
        cost_estimate=pl.CostEstimate(
            flops=8 * planes * owned * flat * flat, bytes_accessed=60 << 20, transcendentals=0
        ),
    )(info, here, phi, halo, band, *blocks)


def dense_rows(cols, blocks, dense):
    def one_block(n, carry):
        i = n // NNZB
        col = cols[i, lax.rem(n, NNZB)]
        dense[pl.ds(pl.multiple_of(i * BLK, BLK), BLK), pl.ds(pl.multiple_of(col * BLK, BLK), BLK)] = (
            blocks[pl.ds(pl.multiple_of(n * BLK, BLK), BLK), :]
        )
        return carry

    lax.fori_loop(0, NB * NNZB, one_block, 0, unroll=4)


def first_kernel(here, k_cols, h_cols, *refs):
    phi, dense_k, product, dense_h, k_blocks, h_blocks, sems = refs[-7:]
    half = (len(refs) - 7) // 2
    depth = refs[0].shape[-2]

    def copies(which):
        stored = refs[which * half : (which + 1) * half]
        target = (k_blocks, h_blocks)[which]
        if half == 1:
            return [pltpu.make_async_copy(stored[0], target, sems.at[which, 0, 0])]
        out_list = []
        columns = SIDES[1] * SIDES[2]
        for n, (block, core, _, column) in enumerate(block_places(here, stored, 1)):
            for z in range(SIDES[0]):
                row = ((core * SIDES[0] + z) * columns + column) * depth
                out_list.append(
                    pltpu.make_async_copy(
                        block.at[z],
                        target.at[pl.ds(pl.multiple_of(row, depth), depth)],
                        sems.at[which, n, z],
                    )
                )
        return out_list

    @pl.when(pl.program_id(0) == 0)
    def _():
        for which in range(2):
            for copy in copies(which):
                copy.start()
        for which, (cols, blocks, dense) in enumerate(
            ((k_cols, k_blocks, dense_k), (h_cols, h_blocks, dense_h))
        ):
            for copy in copies(which):
                copy.wait()
            dense_rows(cols, blocks, dense)

    kphi = jnp.dot(dense_k[...], phi[...], preferred_element_type=jnp.float32)
    product[...] = jnp.dot(
        dense_h[...], kphi.astype(jnp.bfloat16), preferred_element_type=jnp.float32
    )


def first_products(here, k_cols, h_cols, k_parts, h_parts, phi):
    width = phi.shape[1]
    tile = min(COLS, width)
    stored = pltpu.VMEM((NB * NNZB * BLK, BLK), jnp.bfloat16)
    grid_spec = pltpu.PrefetchScalarGridSpec(
        num_scalar_prefetch=3,
        grid=(width // tile,),
        in_specs=[pl.BlockSpec(memory_space=pl.ANY)] * (2 * len(k_parts))
        + [pl.BlockSpec((NF, tile), lambda i, *s: (0, i))],
        out_specs=[
            pl.BlockSpec((NF, NF), lambda i, *s: (0, 0)),
            pl.BlockSpec((NF, tile), lambda i, *s: (0, i)),
        ],
        scratch_shapes=[
            pltpu.VMEM((NF, NF), jnp.bfloat16),
            stored,
            stored,
            pltpu.SemaphoreType.DMA((2, len(k_parts), SIDES[0])),
        ],
    )
    return pl.pallas_call(
        first_kernel,
        out_shape=[
            jax.ShapeDtypeStruct((NF, NF), jnp.bfloat16),
            jax.ShapeDtypeStruct((NF, width), jnp.float32),
        ],
        grid_spec=grid_spec,
        compiler_params=pltpu.CompilerParams(vmem_limit_bytes=VMEM),
        name="products",
        cost_estimate=pl.CostEstimate(
            flops=4 * NF * NF * width, bytes_accessed=24 << 20, transcendentals=0
        ),
    )(here, k_cols, h_cols, *k_parts, *h_parts, phi)


def last_kernel(dense_k, hphi, product, out):
    ydiff = (hphi[...].astype(jnp.float32) - product[...]).astype(jnp.bfloat16)
    out[...] = jnp.dot(dense_k[...], ydiff, preferred_element_type=jnp.float32).astype(jnp.bfloat16)


def last_product(dense_k, hphi, product):
    width = hphi.shape[1]
    tile = min(COLS, width)
    columns = pl.BlockSpec((NF, tile), lambda i: (0, i))
    return pl.pallas_call(
        last_kernel,
        out_shape=jax.ShapeDtypeStruct((NF, width), jnp.bfloat16),
        grid=(width // tile,),
        in_specs=[pl.BlockSpec((NF, NF), lambda i: (0, 0)), columns, columns],
        out_specs=columns,
        compiler_params=pltpu.CompilerParams(vmem_limit_bytes=VMEM),
        name="gradient",
        cost_estimate=pl.CostEstimate(
            flops=2 * NF * NF * width, bytes_accessed=17 << 20, transcendentals=0
        ),
    )(dense_k, hphi, product)


def place_of():
    me = lax.axis_index("func")
    return me // 4, (me // 2) % 2, me % 2


def along_z(part):
    z = place_of()[0]
    n = lax.axis_size("func")
    held = [part]
    for k in range(1, 4):
        held.append(lax.ppermute(part, "func", [(i, (i + 4 * k) % n) for i in range(n)]))

    def at(level):
        taken = held[0]
        for k in range(1, 4):
            taken = jnp.where((z - level) % 4 == k, held[k], taken)
        return taken

    return jnp.stack([at(level) for level in range(4)])


def swapped(block, bit):
    n = lax.axis_size("func")
    return lax.ppermute(block, "func", [(i, i ^ bit) for i in range(n)])


def ordered(lines, near, far, first=0):
    blocks = []
    for p, (line, close, (apart, corner)) in enumerate(zip(lines, near, far)):
        middle = [close, apart] if (p + first) % 2 == 0 else [apart, close]
        blocks += [line, *middle, corner]
    return blocks


def other_core(block):
    return lax.ppermute(block, "rep", [(0, 1), (1, 0)])


def shards(orbitals, centres, potential, kernel, kernel_cols, hamiltonian, intersection_cols):
    rep = lax.axis_index("rep")
    n_func = lax.axis_size("func")
    n_rep = lax.axis_size("rep")
    owned, planes, flat = orbitals.shape
    z_planes, x_size, y_size = potential.shape
    shares = n_func // planes
    width = flat // shares
    x_blocks = x_size // n_rep // ROWS

    def exchange(rows):
        return lax.all_to_all(rows, "func", split_axis=0, concat_axis=0, tiled=True)

    def cut(plane_rows):
        pieces = plane_rows.reshape(planes, owned, shares, width).transpose(0, 2, 1, 3)
        return pieces.reshape(n_func, owned, width)

    half = lax.dynamic_slice_in_dim(potential, rep * (x_size // n_rep), x_size // n_rep, axis=1)
    half = half.astype(jnp.bfloat16).reshape(z_planes, x_blocks, ROWS, y_size).transpose(1, 0, 2, 3)
    phi_planes = orbitals.transpose(1, 0, 2)
    phi_cut = cut(phi_planes)
    edge = jnp.where(rep == 0, phi_planes[planes - 2 :], phi_planes[:2])
    halo = lax.ppermute(edge, "rep", [(0, 1), (1, 0)])
    info = jnp.concatenate([centres[:, :1] + planes * rep, centres[:, 1:]], axis=1)
    info = info.astype(jnp.int32)
    band = planar_band()

    resident = n_func == SIDES[0] * SIDES[1] * SIDES[2]
    if resident:
        _, y, x = place_of()
        here = jnp.stack([rep, y, x]).astype(jnp.int32)
        per = x_blocks // PIECES
        lines = [along_z(half[p * per : (p + 1) * per]) for p in range(PIECES)]
        lines, kernel, hamiltonian, halo, band, info, phi_cut = lax.optimization_barrier(
            (lines, kernel, hamiltonian, halo, band, info, phi_cut)
        )
        near = [swapped(lines[p], 1 + p) for p in range(PIECES)]
        matrix_lines = [along_z(stored[0]) for stored in (kernel, hamiltonian)]
        far = [(swapped(lines[p], 2 - p), swapped(near[p], 2 - p)) for p in range(PIECES)]
        pot = ordered(lines, near, far)
        matrix_near = [swapped(matrix_lines[p], 1 + p) for p in range(2)]
        pot, matrix_lines, matrix_near, phi_cut = lax.optimization_barrier((pot, matrix_lines, matrix_near, phi_cut))
        phi_pts = exchange(phi_cut)
        matrix_far = [
            (swapped(matrix_lines[p], 2 - p), swapped(matrix_near[p], 2 - p)) for p in range(2)
        ]
        pot = pot + [other_core(block) for block in pot]
    else:
        here = jnp.stack([rep, rep, rep]).astype(jnp.int32)
        pot = lax.all_gather(half, ("rep", "func"), axis=0, tiled=False)
        pot = pot.reshape(n_rep, n_func, x_blocks, z_planes, ROWS, y_size)
        pot = pot.transpose(0, 2, 1, 3, 4, 5)
        pot = [pot.reshape(n_rep, x_blocks, n_func * z_planes, ROWS, y_size)]
        phi_pts = exchange(phi_cut)
        k_parts, h_parts = (
            [lax.all_gather(stored, ("rep", "func"), axis=1, tiled=True).reshape(-1, BLK)]
            for stored in (kernel, hamiltonian)
        )

    extra = -owned % GROUP
    padded = [
        jnp.pad(info, ((0, extra), (0, 0))),
        jnp.pad(phi_planes, ((0, 0), (0, extra), (0, 0))),
        jnp.pad(halo, ((0, 0), (0, extra), (0, 0))),
    ]
    info, phi_planes, halo = padded
    hphi = make_hphi(info, here, phi_planes, halo, band, pot, resident)[:, :owned]
    if resident:
        hphi, matrix_far = lax.optimization_barrier((hphi, matrix_far))
        k_parts, h_parts = (
            ordered(matrix_lines[p : p + 1], matrix_near[p : p + 1], matrix_far[p : p + 1], p)
            for p in range(2)
        )
        k_parts = k_parts + [other_core(block) for block in k_parts]
        h_parts = h_parts + [other_core(block) for block in h_parts]
    phi_pts = phi_pts.reshape(n_func * owned, width)
    dense_k, product = first_products(
        here, kernel_cols, intersection_cols, k_parts, h_parts, phi_pts
    )
    hphi_pts = exchange(cut(hphi)).reshape(n_func * owned, width)
    gradient = last_product(dense_k, hphi_pts, product)
    back = exchange(gradient.reshape(n_func, owned, width))
    back = back.reshape(planes, shares, owned, width).transpose(2, 0, 1, 3)
    return back.reshape(owned, planes, flat)


def solution(mesh):
    placed = (
        P("func", "rep", None),
        P("func", None),
        P("func", None, None),
        P("rep", "func", None),
        P(),
        P("rep", "func", None),
        P(),
    )
    return jax.shard_map(
        shards, mesh=mesh, in_specs=placed, out_specs=P("func", "rep", None), check_vma=False
    )
```

```python
import functools

import jax
import jax.numpy as jnp
from jax import lax
from jax.experimental import pallas as pl
from jax.experimental.pallas import tpu as pltpu
from jax.sharding import PartitionSpec as P

BOX = 32
BLK = 128
NNZB = 12
NB = 12
NF = NB * BLK
LANES = 128
ROWS = 16
GROUP = 16
COLS = 256
VMEM = 56 * 1024 * 1024
SLOTS = 8
PIECES = 2

CENTRE = 90.0
NEAR = -16.0
FAR = 1.0
SCALE = 1.0 / 96.0


SIDES = (4, 2, 2)


def block_places(here, blocks, pieces=PIECES):
    rep, y, x = (here[k] for k in range(3))
    places = []
    for n, block in enumerate(blocks):
        core = rep if n < len(blocks) // 2 else 1 - rep
        piece = n // 4 % pieces
        to_y = y if n % 4 < 2 else 1 - y
        to_x = x if n % 2 == 0 else 1 - x
        places.append((block, core, piece, to_y * SIDES[2] + to_x))
    return places


def planar_band():
    row = lax.broadcasted_iota(jnp.int32, (2 * COLS, COLS), 0) - LANES
    col = lax.broadcasted_iota(jnp.int32, (2 * COLS, COLS), 1)
    across = jnp.abs((row + LANES) // BOX - (col + LANES) // BOX)
    along = jnp.abs((row + LANES) % BOX - (col + LANES) % BOX)
    band = jnp.zeros((2 * COLS, COLS), jnp.float32)
    for one, other in ((across, along), (along, across)):
        band = jnp.where((one == 0) & (other == 1), NEAR, band)
        band = jnp.where((one == 0) & (other == 2), FAR, band)
    band = jnp.where((across == 0) & (along == 0), CENTRE, band)
    return band.astype(jnp.bfloat16)


def hphi_kernel(info, here, phi, halo, band, *refs, resident):
    planes, group, flat = phi.shape
    step = pl.program_id(0)
    total = pl.num_programs(0) * group
    span = 3 * ROWS
    flag = here[0].astype(jnp.float32)
    if resident:
        blocks, (out, pot, rows, win, sems) = refs[:-5], refs[-5:]
    else:
        pot, out, buf, rows, win, sems = refs
    x_blocks = pot.shape[1]

    def copies(index, slot):
        z = info[index, 0]
        first = info[index, 1] // ROWS
        out_list = []
        for k in range(3):
            block = lax.rem(first + k, 2 * x_blocks)
            out_list.append(
                pltpu.make_async_copy(
                    pot.at[block // x_blocks, lax.rem(block, x_blocks), pl.ds(z, planes)],
                    buf.at[slot, k],
                    sems.at[slot, k],
                )
            )
        return out_list

    @pl.when(step == 0)
    def _():
        if resident:
            started = []
            for n, (block, core, piece, column) in enumerate(block_places(here, blocks)):
                per, depth = block.shape[1:3]
                for z in range(SIDES[0]):
                    target = pl.multiple_of((z * SIDES[1] * SIDES[2] + column) * depth, depth)
                    started.append(
                        pltpu.make_async_copy(
                            block.at[z],
                            pot.at[core, pl.ds(piece * per, per), pl.ds(target, depth)],
                            sems.at[n, z],
                        )
                    )
            for copy in started:
                copy.start()
            for copy in started:
                copy.wait()
        else:
            for early in range(SLOTS - 1):
                for copy in copies(early, early):
                    copy.start()

    lane = lax.broadcasted_iota(jnp.int32, (8, LANES), 1)

    def one_function(f, carry):
        index = step * group + f
        if resident:
            z0 = info[index, 0]
            first = info[index, 1] // ROWS
            for k in range(3):
                block = lax.rem(first + k, 2 * x_blocks)
                source = pot.at[block // x_blocks, lax.rem(block, x_blocks)]
                for z in range(planes):
                    rows[pl.ds(z * span + k * ROWS, ROWS), :] = source[z0 + z].astype(jnp.float32)
        else:
            slot = lax.rem(index, SLOTS)
            ahead = index + SLOTS - 1

            @pl.when(ahead < total)
            def _():
                for copy in copies(ahead, lax.rem(ahead, SLOTS)):
                    copy.start()

            for copy in copies(index, slot):
                copy.wait()
            for z in range(planes):
                for k in range(3):
                    rows[pl.ds(z * span + k * ROWS, ROWS), :] = buf[slot, k, z].astype(jnp.float32)
        shift_x = lax.rem(info[index, 1], ROWS)
        shift_y = info[index, 2]
        for z in range(planes):
            value = None
            for b in range(4):
                part = rows[pl.ds(z * span + b + shift_x, 8, stride=4), :]
                part = pltpu.roll(part, lax.rem(b * BOX + LANES - shift_y, LANES), axis=1)
                value = part if value is None else jnp.where(lane >= b * BOX, part, value)
            win[pl.ds(z * group + f, 8, stride=planes * group), :] = value
        return carry

    lax.fori_loop(0, group, one_function, 0)

    pieces = flat // COLS
    for c in range(pieces):
        low = max(0, c * COLS - LANES)
        high = min(flat, c * COLS + COLS + LANES)
        cols = slice(c * COLS, (c + 1) * COLS)
        left = phi[:, :, low:high].reshape(planes * group, high - low)
        base = low - (c * COLS - LANES)
        planar = jnp.dot(
            left, band[base : base + high - low, :], preferred_element_type=jnp.float32
        )
        level = [phi[z, :, cols].astype(jnp.float32) for z in range(planes)]
        other = [halo[h, :, cols].astype(jnp.float32) for h in range(2)]
        below = [h * flag for h in other]
        above = [h * (1.0 - flag) for h in other]
        level = below + level + above
        for z in range(planes):
            kin = planar[z * group : (z + 1) * group]
            kin = kin + NEAR * (level[z + 1] + level[z + 3]) + FAR * (level[z] + level[z + 4])
            w = jnp.concatenate(
                [
                    win[pl.ds((a * planes + z) * group, group), :]
                    for a in range(c * COLS // LANES, (c + 1) * COLS // LANES)
                ],
                axis=1,
            )
            vphi = (w * level[z + 2]).astype(jnp.bfloat16).astype(jnp.float32)
            out[z, :, cols] = (SCALE * kin + vphi).astype(jnp.bfloat16)


def make_hphi(info, here, phi, halo, band, blocks, resident):
    planes, owned, flat = phi.shape
    span = 3 * ROWS
    if resident:
        per, depth = blocks[0].shape[1:3]
        size = (2, PIECES * per, SIDES[0] * SIDES[1] * SIDES[2] * depth, ROWS, LANES)
        taken = pltpu.VMEM(size, jnp.bfloat16)
        sems = pltpu.SemaphoreType.DMA((len(blocks), SIDES[0]))
    else:
        taken = pltpu.VMEM((SLOTS, 3, planes, ROWS, LANES), jnp.bfloat16)
        sems = pltpu.SemaphoreType.DMA((SLOTS, 3))
    grid_spec = pltpu.PrefetchScalarGridSpec(
        num_scalar_prefetch=2,
        grid=(owned // GROUP,),
        in_specs=[
            pl.BlockSpec((planes, GROUP, flat), lambda i, s, t: (0, i, 0)),
            pl.BlockSpec((2, GROUP, flat), lambda i, s, t: (0, i, 0)),
            pl.BlockSpec(band.shape, lambda i, s, t: (0, 0)),
        ]
        + [pl.BlockSpec(memory_space=pl.ANY)] * len(blocks),
        out_specs=pl.BlockSpec((planes, GROUP, flat), lambda i, s, t: (0, i, 0)),
        scratch_shapes=[
            taken,
            pltpu.VMEM((planes * span, LANES), jnp.float32),
            pltpu.VMEM((flat // LANES * planes * GROUP, LANES), jnp.float32),
            sems,
        ],
    )
    return pl.pallas_call(
        functools.partial(hphi_kernel, resident=resident),
        out_shape=jax.ShapeDtypeStruct((planes, owned, flat), jnp.bfloat16),
        grid_spec=grid_spec,
        compiler_params=pltpu.CompilerParams(vmem_limit_bytes=VMEM),
        name="hphi",
        cost_estimate=pl.CostEstimate(
            flops=8 * planes * owned * flat * flat, bytes_accessed=60 << 20, transcendentals=0
        ),
    )(info, here, phi, halo, band, *blocks)


def dense_rows(cols, blocks, dense):
    def one_block(n, carry):
        i = n // NNZB
        col = cols[i, lax.rem(n, NNZB)]
        dense[pl.ds(pl.multiple_of(i * BLK, BLK), BLK), pl.ds(pl.multiple_of(col * BLK, BLK), BLK)] = (
            blocks[pl.ds(pl.multiple_of(n * BLK, BLK), BLK), :]
        )
        return carry

    lax.fori_loop(0, NB * NNZB, one_block, 0, unroll=4)


def first_kernel(here, k_cols, h_cols, *refs):
    phi, dense_k, product, dense_h, k_blocks, h_blocks, sems = refs[-7:]
    half = (len(refs) - 7) // 2
    depth = refs[0].shape[-2]

    def copies(which):
        stored = refs[which * half : (which + 1) * half]
        target = (k_blocks, h_blocks)[which]
        if half == 1:
            return [pltpu.make_async_copy(stored[0], target, sems.at[which, 0, 0])]
        out_list = []
        columns = SIDES[1] * SIDES[2]
        for n, (block, core, _, column) in enumerate(block_places(here, stored, 1)):
            for z in range(SIDES[0]):
                row = ((core * SIDES[0] + z) * columns + column) * depth
                out_list.append(
                    pltpu.make_async_copy(
                        block.at[z],
                        target.at[pl.ds(pl.multiple_of(row, depth), depth)],
                        sems.at[which, n, z],
                    )
                )
        return out_list

    @pl.when(pl.program_id(0) == 0)
    def _():
        for which in range(2):
            for copy in copies(which):
                copy.start()
        for which, (cols, blocks, dense) in enumerate(
            ((k_cols, k_blocks, dense_k), (h_cols, h_blocks, dense_h))
        ):
            for copy in copies(which):
                copy.wait()
            dense_rows(cols, blocks, dense)

    kphi = jnp.dot(dense_k[...], phi[...], preferred_element_type=jnp.float32)
    product[...] = jnp.dot(
        dense_h[...], kphi.astype(jnp.bfloat16), preferred_element_type=jnp.float32
    )


def first_products(here, k_cols, h_cols, k_parts, h_parts, phi):
    width = phi.shape[1]
    tile = min(COLS, width)
    stored = pltpu.VMEM((NB * NNZB * BLK, BLK), jnp.bfloat16)
    grid_spec = pltpu.PrefetchScalarGridSpec(
        num_scalar_prefetch=3,
        grid=(width // tile,),
        in_specs=[pl.BlockSpec(memory_space=pl.ANY)] * (2 * len(k_parts))
        + [pl.BlockSpec((NF, tile), lambda i, *s: (0, i))],
        out_specs=[
            pl.BlockSpec((NF, NF), lambda i, *s: (0, 0)),
            pl.BlockSpec((NF, tile), lambda i, *s: (0, i)),
        ],
        scratch_shapes=[
            pltpu.VMEM((NF, NF), jnp.bfloat16),
            stored,
            stored,
            pltpu.SemaphoreType.DMA((2, len(k_parts), SIDES[0])),
        ],
    )
    return pl.pallas_call(
        first_kernel,
        out_shape=[
            jax.ShapeDtypeStruct((NF, NF), jnp.bfloat16),
            jax.ShapeDtypeStruct((NF, width), jnp.float32),
        ],
        grid_spec=grid_spec,
        compiler_params=pltpu.CompilerParams(vmem_limit_bytes=VMEM),
        name="products",
        cost_estimate=pl.CostEstimate(
            flops=4 * NF * NF * width, bytes_accessed=24 << 20, transcendentals=0
        ),
    )(here, k_cols, h_cols, *k_parts, *h_parts, phi)


def last_kernel(dense_k, hphi, product, out):
    ydiff = (hphi[...].astype(jnp.float32) - product[...]).astype(jnp.bfloat16)
    out[...] = jnp.dot(dense_k[...], ydiff, preferred_element_type=jnp.float32).astype(jnp.bfloat16)


def last_product(dense_k, hphi, product):
    width = hphi.shape[1]
    tile = min(COLS, width)
    columns = pl.BlockSpec((NF, tile), lambda i: (0, i))
    return pl.pallas_call(
        last_kernel,
        out_shape=jax.ShapeDtypeStruct((NF, width), jnp.bfloat16),
        grid=(width // tile,),
        in_specs=[pl.BlockSpec((NF, NF), lambda i: (0, 0)), columns, columns],
        out_specs=columns,
        compiler_params=pltpu.CompilerParams(vmem_limit_bytes=VMEM),
        name="gradient",
        cost_estimate=pl.CostEstimate(
            flops=2 * NF * NF * width, bytes_accessed=17 << 20, transcendentals=0
        ),
    )(dense_k, hphi, product)


def place_of():
    me = lax.axis_index("func")
    return me // 4, (me // 2) % 2, me % 2


def along_z(part):
    z = place_of()[0]
    n = lax.axis_size("func")
    held = [part]
    for k in range(1, 4):
        held.append(lax.ppermute(part, "func", [(i, (i + 4 * k) % n) for i in range(n)]))

    def at(level):
        taken = held[0]
        for k in range(1, 4):
            taken = jnp.where((z - level) % 4 == k, held[k], taken)
        return taken

    return jnp.stack([at(level) for level in range(4)])


def swapped(block, bit):
    n = lax.axis_size("func")
    return lax.ppermute(block, "func", [(i, i ^ bit) for i in range(n)])


def ordered(lines, near, far, first=0):
    blocks = []
    for p, (line, close, (apart, corner)) in enumerate(zip(lines, near, far)):
        middle = [close, apart] if (p + first) % 2 == 0 else [apart, close]
        blocks += [line, *middle, corner]
    return blocks


def other_core(block):
    return lax.ppermute(block, "rep", [(0, 1), (1, 0)])


def shards(orbitals, centres, potential, kernel, kernel_cols, hamiltonian, intersection_cols):
    rep = lax.axis_index("rep")
    n_func = lax.axis_size("func")
    n_rep = lax.axis_size("rep")
    owned, planes, flat = orbitals.shape
    z_planes, x_size, y_size = potential.shape
    shares = n_func // planes
    width = flat // shares
    x_blocks = x_size // n_rep // ROWS

    def exchange(rows):
        return lax.all_to_all(rows, "func", split_axis=0, concat_axis=0, tiled=True)

    def cut(plane_rows):
        pieces = plane_rows.reshape(planes, owned, shares, width).transpose(0, 2, 1, 3)
        return pieces.reshape(n_func, owned, width)

    half = lax.dynamic_slice_in_dim(potential, rep * (x_size // n_rep), x_size // n_rep, axis=1)
    half = half.astype(jnp.bfloat16).reshape(z_planes, x_blocks, ROWS, y_size).transpose(1, 0, 2, 3)
    phi_planes = orbitals.transpose(1, 0, 2)
    phi_cut = cut(phi_planes)
    edge = jnp.where(rep == 0, phi_planes[planes - 2 :], phi_planes[:2])
    halo = lax.ppermute(edge, "rep", [(0, 1), (1, 0)])
    info = jnp.concatenate([centres[:, :1] + planes * rep, centres[:, 1:]], axis=1)
    info = info.astype(jnp.int32)
    band = planar_band()

    resident = n_func == SIDES[0] * SIDES[1] * SIDES[2]
    if resident:
        _, y, x = place_of()
        here = jnp.stack([rep, y, x]).astype(jnp.int32)
        per = x_blocks // PIECES
        lines = [along_z(half[p * per : (p + 1) * per]) for p in range(PIECES)]
        lines, kernel, hamiltonian, halo, band, info, phi_cut = lax.optimization_barrier(
            (lines, kernel, hamiltonian, halo, band, info, phi_cut)
        )
        near = [swapped(lines[p], 1 + p) for p in range(PIECES)]
        matrix_lines = [along_z(stored[0]) for stored in (kernel, hamiltonian)]
        far = [(swapped(lines[p], 2 - p), swapped(near[p], 2 - p)) for p in range(PIECES)]
        pot = ordered(lines, near, far)
        pot, matrix_lines, phi_cut = lax.optimization_barrier((pot, matrix_lines, phi_cut))
        pot = pot + [other_core(block) for block in pot]
        phi_pts = exchange(phi_cut)
        matrix_near = [swapped(matrix_lines[p], 1 + p) for p in range(2)]
    else:
        here = jnp.stack([rep, rep, rep]).astype(jnp.int32)
        pot = lax.all_gather(half, ("rep", "func"), axis=0, tiled=False)
        pot = pot.reshape(n_rep, n_func, x_blocks, z_planes, ROWS, y_size)
        pot = pot.transpose(0, 2, 1, 3, 4, 5)
        pot = [pot.reshape(n_rep, x_blocks, n_func * z_planes, ROWS, y_size)]
        phi_pts = exchange(phi_cut)
        k_parts, h_parts = (
            [lax.all_gather(stored, ("rep", "func"), axis=1, tiled=True).reshape(-1, BLK)]
            for stored in (kernel, hamiltonian)
        )

    extra = -owned % GROUP
    padded = [
        jnp.pad(info, ((0, extra), (0, 0))),
        jnp.pad(phi_planes, ((0, 0), (0, extra), (0, 0))),
        jnp.pad(halo, ((0, 0), (0, extra), (0, 0))),
    ]
    info, phi_planes, halo = padded
    hphi = make_hphi(info, here, phi_planes, halo, band, pot, resident)[:, :owned]
    if resident:
        hphi, matrix_near = lax.optimization_barrier((hphi, matrix_near))
        matrix_far = [
            (swapped(matrix_lines[p], 2 - p), swapped(matrix_near[p], 2 - p)) for p in range(2)
        ]
        sides = [pair[0] for pair in matrix_far]
        hphi, sides = lax.optimization_barrier((hphi, sides))
        matrix_far = [(side, pair[1]) for side, pair in zip(sides, matrix_far)]
        k_parts, h_parts = (
            ordered(matrix_lines[p : p + 1], matrix_near[p : p + 1], matrix_far[p : p + 1], p)
            for p in range(2)
        )
        k_parts = k_parts + [other_core(block) for block in k_parts]
        h_parts = h_parts + [other_core(block) for block in h_parts]
    phi_pts = phi_pts.reshape(n_func * owned, width)
    dense_k, product = first_products(
        here, kernel_cols, intersection_cols, k_parts, h_parts, phi_pts
    )
    hphi_pts = exchange(cut(hphi)).reshape(n_func * owned, width)
    gradient = last_product(dense_k, hphi_pts, product)
    back = exchange(gradient.reshape(n_func, owned, width))
    back = back.reshape(planes, shares, owned, width).transpose(2, 0, 1, 3)
    return back.reshape(owned, planes, flat)


def solution(mesh):
    placed = (
        P("func", "rep", None),
        P("func", None),
        P("func", None, None),
        P("rep", "func", None),
        P(),
        P("rep", "func", None),
        P(),
    )
    return jax.shard_map(
        shards, mesh=mesh, in_specs=placed, out_specs=P("func", "rep", None), check_vma=False
    )
```
